32 devices in a mesh: groups: 2 (over y), rep: 4 (over z), tp: 4 (over x, core).
Axes of the slice: x: 2, y: 2, z: 4, core: 2. Of those that a mesh axis runs over, the one named last changes fastest.
Arguments:
- hidden: bfloat16 [1024, 8192], P(('groups', 'rep'), 'tp'), parts along dimension 0, may hold values from -6 to 6
- queries: bfloat16 [1024, 8192], P(('groups', 'rep'), 'tp'), parts along dimension 0, may hold values from -5 to 5
- fresh_token_keys: bfloat16 [1024, 1024], P(('groups', 'rep'), 'tp'), parts along dimension 0, may hold values from -5 to 5
- cached_key_rows: bfloat16 [1024, 32, 1024], P(('groups', 'rep'), None, 'tp'), parts along dimension 0, may hold values from -5 to 5
- cached_value_rows: bfloat16 [1024, 32, 1024], P(('groups', 'rep'), None, 'tp'), parts along dimension 0, may hold values from -6 to 6
- lengths: int32 [1024], P(('groups', 'rep')), parts along dimension 0, may hold values from 1 to 32, as said below
- row_adapter_index: int32 [1024], P(('groups', 'rep')), parts along dimension 0, may hold values from 0 to 127, as said below
- adapter_table_place: int32 [256], P('groups'), parts along dimension 0, may hold values from 0 to 127, as said below
- value_projection_matrix: bfloat16 [8192, 1024], P(None, 'tp'), may hold values from -0.0625 to 0.0625
- adapter_down_factor: bfloat16 [256, 16, 8192], P(('groups', 'rep'), None, 'tp'), parts along dimension 0, may hold values from -0.0625 to 0.0625
- adapter_up_factor: bfloat16 [256, 16, 1024], P(('groups', 'rep'), None, 'tp'), parts along dimension 0, may hold values from -1.5 to 1.5
Outputs:
- value_new: bfloat16 [1024, 1024], P(('groups', 'rep'), 'tp'), parts along dimension 0
- attended: bfloat16 [1024, 8192], P(('groups', 'rep'), 'tp'), parts along dimension 0
The draws below stay inside these ranges and needn't reach their ends.
There are 2 independent parts, one for each index of `groups`. The reference program is written for one: setup_inputs(seed, part) draws one part's arguments, and reference() takes and returns one part's arrays. A program takes and returns all parts, laid end to end along the dimension named above; an argument that names none is the same for every part. Nothing has to cross between parts.
Inputs may be any that keep to these rules, and one draw needn't show every extreme that they name: `row_adapter_index`: at most 64 of the 128 rows of one index of rep use adapters a whose adapter_table_place[a] // 32 is one and the same index of rep; some index of rep receives exactly 64 such rows from every index of rep. `adapter_table_place`: A permutation of the adapters. `lengths`: some row holds 32 live positions.
All inputs are finite; a program needn't handle non-finite values.
Results may differ from the reference program's by a relative error of at most 0.01.
Values may be sent and summed in bfloat16 or wider, within the bound.
A program may use at most 64 MiB of HBM per device.

```python
import jax
import jax.numpy as jnp
from jax import lax

MODEL_WIDTH = 8192
HEADS = 64
KV_HEADS = 8
HD = 128
ADAPTER_RANK = 16
ADP_DEV = 32
ROWS_DEV = 128
CACHE = 32
ADAPTER_COUNT = 128
ROWS = 512
CAP = 64
QW = 8192
VALUE_FEATURES = 1024


def slot_order(key):
    return jax.random.permutation(key, ADAPTER_COUNT).astype(jnp.int32)


def draw_adapter_table_place(key, part):
    order = slot_order(key)
    return jnp.argsort(order).astype(jnp.int32)


def draw_row_adapter_index(key, part):
    order = slot_order(key)
    key = jax.random.fold_in(key, 5)
    replicas = ADAPTER_COUNT // ADP_DEV
    blocks = ROWS // ROWS_DEV
    first, second = jax.random.split(key)
    hottest = jax.random.randint(first, (), 0, replicas)

    def one_block(block_key):
        key_a, key_b, key_c, key_d = jax.random.split(block_key, 4)
        others = jax.random.permutation(key_a, (replicas - 1) * CAP)[:ROWS_DEV - CAP]
        target = jnp.concatenate([jnp.full((CAP,), hottest, jnp.int32), ((hottest + 1 + others // CAP) % replicas).astype(jnp.int32)])
        target = jax.random.permutation(key_b, target)
        inner = jnp.minimum(jax.random.randint(key_c, (ROWS_DEV,), 0, ADP_DEV), jax.random.randint(key_d, (ROWS_DEV,), 0, ADP_DEV))
        return (target * ADP_DEV + inner).astype(jnp.int32)
    table_places = jax.vmap(one_block)(jax.random.split(second, blocks)).reshape(ROWS)
    return order[table_places]


def draw_lengths(key, part):
    key = jax.random.fold_in(key, 7)
    first, second = jax.random.split(key)
    values = jax.random.randint(first, (ROWS,), 1, CACHE + 1)
    fullrow = jax.random.randint(second, (), 0, ROWS)
    return jnp.where(jnp.arange(ROWS) == fullrow, CACHE, values).astype(jnp.int32)


def draw_queries(key, part):
    key = jax.random.fold_in(key, 11)
    values = jnp.clip(jax.random.normal(key, (ROWS, QW), jnp.float32), -5.0, 5.0)
    return values.astype(jnp.bfloat16)


def draw_fresh_token_keys(key, part):
    key = jax.random.fold_in(key, 13)
    values = jnp.clip(jax.random.normal(key, (ROWS, VALUE_FEATURES), jnp.float32), -5.0, 5.0)
    return values.astype(jnp.bfloat16)


def draw_cached_key_rows(key, part):
    key = jax.random.fold_in(key, 17)
    values = jnp.clip(jax.random.normal(key, (ROWS, CACHE, VALUE_FEATURES), jnp.float32), -5.0, 5.0)
    return values.astype(jnp.bfloat16)


def block_scale(key, dims, cuts, smallest, high):
    gain, own = 1.0, jax.random.fold_in(key, 6)
    for axis_at, blocks in cuts:
        steps = jnp.exp(jax.random.uniform(jax.random.fold_in(own, axis_at), (blocks,), jnp.float32, smallest / len(cuts), high / len(cuts)))
        gain = gain * jnp.repeat(steps, dims[axis_at] // blocks).reshape([-1 if axis == axis_at else 1 for axis in range(len(dims))])
    return gain


def centred(rng, shape, scale, reach, shards=(), kind=jnp.bfloat16):
    result = jax.random.normal(rng, shape, jnp.float32) * scale
    if len(shards) > 0:
        result = block_scale(rng, shape, shards, -0.22, 0.18) * result
    return jnp.clip(result, min=-reach, max=reach).astype(kind)


def setup_inputs(seed: int = 0, part: int = 0) -> dict:
    streams_of = jax.random.split(jax.random.key(seed), 12)
    part_splits = jax.random.split(jax.random.fold_in(streams_of[11], part), 12)
    return {
        "hidden": centred(part_splits[0], (ROWS, MODEL_WIDTH), 1.0, 6.0, ((0, 4), (1, 4))),
        "queries": draw_queries(jax.random.fold_in(jax.random.fold_in(streams_of[11], part), 71), part),
        "fresh_token_keys": draw_fresh_token_keys(jax.random.fold_in(jax.random.fold_in(streams_of[11], part), 71), part),
        "cached_key_rows": draw_cached_key_rows(jax.random.fold_in(jax.random.fold_in(streams_of[11], part), 71), part),
        "cached_value_rows": centred(part_splits[4], (ROWS, CACHE, VALUE_FEATURES), 1.0, 6.0, ((0, 4), (2, 4))),
        "lengths": draw_lengths(jax.random.fold_in(jax.random.fold_in(streams_of[11], part), 71), part),
        "row_adapter_index": draw_row_adapter_index(jax.random.fold_in(jax.random.fold_in(streams_of[11], part), 71), part),
        "adapter_table_place": draw_adapter_table_place(jax.random.fold_in(jax.random.fold_in(streams_of[11], part), 71), part),
        "value_projection_matrix": centred(streams_of[8], (MODEL_WIDTH, VALUE_FEATURES), MODEL_WIDTH ** -0.5, 0.0625, ((1, 4),)),
        "adapter_down_factor": centred(part_splits[9], (ADAPTER_COUNT, ADAPTER_RANK, MODEL_WIDTH), MODEL_WIDTH ** -0.5, 0.0625, ((0, 4), (2, 4))),
        "adapter_up_factor": centred(part_splits[10], (ADAPTER_COUNT, ADAPTER_RANK, VALUE_FEATURES), ADAPTER_RANK ** -0.5, 1.5, ((0, 4), (2, 4))),
    }


adapter_scale = 2.0


def reference(hidden, queries, fresh_token_keys, cached_key_rows, cached_value_rows, lengths, row_adapter_index, adapter_table_place, value_projection_matrix, adapter_down_factor, adapter_up_factor):
    base = jnp.dot(hidden, value_projection_matrix, preferred_element_type=jnp.float32)
    table_places = jnp.take(adapter_table_place, row_adapter_index).astype(jnp.int32)

    def shrink_block(pair):
        rows_in, lookup_position = pair
        factor_pairs = jnp.take(adapter_down_factor, lookup_position, axis=0).astype(jnp.float32)
        return jnp.einsum("rd,rkd->rk", rows_in.astype(jnp.float32), factor_pairs)

    reduced_input = lax.map(shrink_block, (hidden.reshape(-1, ROWS_DEV, MODEL_WIDTH), table_places.reshape(-1, ROWS_DEV)))
    reduced_input = reduced_input.reshape(ROWS, ADAPTER_RANK).astype(jnp.bfloat16)
    upper_bound = jnp.take(adapter_up_factor, table_places, axis=0).astype(jnp.float32)
    adapter_update = (adapter_scale * jnp.einsum("mo,mol->ml", reduced_input.astype(jnp.float32), upper_bound)).astype(jnp.bfloat16)
    value_new = (base + adapter_update.astype(jnp.float32)).astype(jnp.bfloat16)

    groups = HEADS // KV_HEADS
    inverse = 1.0 / (HD ** 0.5)
    query_heads = queries.astype(jnp.float32).reshape(ROWS, KV_HEADS, groups, HD)
    key_heads = cached_key_rows.astype(jnp.float32).reshape(ROWS, CACHE, KV_HEADS, HD)
    value_heads = cached_value_rows.astype(jnp.float32).reshape(ROWS, CACHE, KV_HEADS, HD)
    scores = jnp.einsum("rghd,rcgd->rghc", query_heads, key_heads) * inverse
    own = jnp.einsum("rghd,rgd->rgh", query_heads, fresh_token_keys.astype(jnp.float32).reshape(ROWS, KV_HEADS, HD)) * inverse
    live = (jnp.arange(CACHE, dtype=jnp.int32)[None, :] < lengths[:, None])[:, None, None, :]
    top = jnp.maximum(jnp.max(jnp.where(live, scores, -jnp.inf), axis=-1), own)
    expo = jnp.where(live, jnp.exp(scores - top[..., None]), 0.0)
    own_expo = jnp.exp(own - top)
    total = jnp.sum(expo, axis=-1) + own_expo
    weights = (expo / total[..., None]).astype(jnp.bfloat16)
    own_weight = (own_expo / total).astype(jnp.bfloat16)
    mixed = jnp.einsum("rghc,rcgd->rghd", weights.astype(jnp.float32), value_heads)
    mixed = mixed + own_weight.astype(jnp.float32)[..., None] * value_new.astype(jnp.float32).reshape(ROWS, KV_HEADS, 1, HD)
    attended = mixed.reshape(ROWS, QW).astype(jnp.bfloat16)
    return value_new, attended
```

```python
import functools

import jax
import jax.numpy as jnp
from jax import lax
from jax.experimental import pallas as pl
from jax.experimental.pallas import tpu as pltpu
from jax.sharding import PartitionSpec as P

HD = 128
ROW_BLOCK = 16
ADAPTER_SCALE = 2.0
MASKED = -1e30
F32, BF16 = jnp.float32, jnp.bfloat16
NT = (((1,), (1,)), ((), ()))
TN = (((0,), (0,)), ((), ()))
NN = (((1,), (0,)), ((), ()))


def dot(a, b, dims=NN):
    return lax.dot_general(a, b, dims, preferred_element_type=F32)


def iota(shape, dim):
    return lax.broadcasted_iota(jnp.int32, shape, dim)


def kernel(
    reps, tps, cap, stored, rank,
    hidden, fresh, lengths, index, places, q_hbm, k_hbm, v_hbm, w_hbm, down_hbm, up_hbm,
    value_out, attended_out,
    q_v, k_v, v_v, w_v, down_v, up_v, local_sem,
    shards, out_rows, in_rows, out_ids, in_ids, slots, part, parts, out_delta, in_delta,
    mixed_v, own_v, length_v, value_v, attended_v,
    gather_send, gather_recv, row_send, row_recv, id_send, id_recv,
    part_send, part_recv, delta_send, delta_recv,
):
    me_r, me_t = lax.axis_index("rep"), lax.axis_index("tp")
    rows, kv_local = hidden.shape[0], fresh.shape[1] // HD
    group = q_v.shape[1] // fresh.shape[1]
    positions = k_v.shape[1]
    span = ROW_BLOCK * positions

    def rep_at(k):
        return lax.rem(me_r + k, reps)

    def tp_at(k):
        return lax.rem(me_t + k, tps)

    sibling = me_t + 1 - 2 * lax.rem(me_t, 2)

    barrier = pltpu.get_barrier_semaphore()

    def greet_rep(k, c):
        pl.semaphore_signal(barrier, inc=1, device_id={"rep": rep_at(k)}, device_id_type=pl.DeviceIdType.MESH)
        return c

    def greet_tp(k, c):
        pl.semaphore_signal(barrier, inc=1, device_id={"tp": tp_at(k)}, device_id_type=pl.DeviceIdType.MESH)
        return c

    lax.fori_loop(1, reps, greet_rep, 0)
    lax.fori_loop(1, tps, greet_tp, 0)

    loads = [
        pltpu.make_async_copy(src, dst, local_sem.at[n])
        for n, (src, dst) in enumerate(
            ((q_hbm, q_v), (k_hbm, k_v), (v_hbm, v_v), (down_hbm, down_v), (w_hbm, w_v), (up_hbm, up_v))
        )
    ]
    for load in loads:
        load.start()

    adapters = places.shape[1]
    place = places[...].astype(F32)
    owner_tab = jnp.floor((place + 0.5) / stored)
    inner_tab = place - owner_tab * stored
    hot = (iota((adapters, rows), 0) == index[...]).astype(F32).astype(BF16)
    owner = dot(jnp.broadcast_to(owner_tab, (8, adapters)).astype(BF16), hot)
    inner = dot(jnp.broadcast_to(inner_tab, (8, adapters)).astype(BF16), hot).astype(BF16)
    rep_pad = max(8, reps)
    owner_row = owner[0:1, :]
    owner_hot = (iota((rep_pad, rows), 0).astype(F32) == owner_row).astype(F32)
    earlier = (iota((rows, rows), 0) < iota((rows, rows), 1)).astype(F32).astype(BF16)
    before = dot(owner_hot.astype(BF16), earlier)
    position = jnp.sum(before * owner_hot, axis=0, keepdims=True)
    slot_iota = iota((rows, rows), 0).astype(F32)

    def gather_copy(src, to, q, n):
        return pltpu.make_async_remote_copy(
            src_ref=src, dst_ref=shards.at[q], send_sem=gather_send.at[n], recv_sem=gather_recv.at[q],
            device_id={"tp": to}, device_id_type=pl.DeviceIdType.MESH,
        )

    def row_copy(d):
        return pltpu.make_async_remote_copy(
            src_ref=out_rows.at[d], dst_ref=in_rows.at[me_r], send_sem=row_send.at[d], recv_sem=row_recv.at[me_r],
            device_id={"rep": d}, device_id_type=pl.DeviceIdType.MESH,
        )

    def id_copy(d):
        return pltpu.make_async_remote_copy(
            src_ref=out_ids.at[d], dst_ref=in_ids.at[me_r], send_sem=id_send.at[d], recv_sem=id_recv.at[me_r],
            device_id={"rep": d}, device_id_type=pl.DeviceIdType.MESH,
        )

    def row_arrival(s):
        return pltpu.make_async_remote_copy(
            src_ref=out_rows.at[s], dst_ref=in_rows.at[s], send_sem=row_send.at[s], recv_sem=row_recv.at[s],
            device_id={"rep": s}, device_id_type=pl.DeviceIdType.MESH,
        )

    def id_arrival(s):
        return pltpu.make_async_remote_copy(
            src_ref=out_ids.at[s], dst_ref=in_ids.at[s], send_sem=id_send.at[s], recv_sem=id_recv.at[s],
            device_id={"rep": s}, device_id_type=pl.DeviceIdType.MESH,
        )

    def fill(d):
        member = jnp.where(owner_row == d.astype(F32), position, -1.0)
        dispatch = (slot_iota == member).astype(F32).astype(BF16)
        slots[d] = dispatch
        return dispatch

    pl.semaphore_wait(barrier, reps - 1 + tps - 1)

    def send_rows(i, c):
        d = rep_at(1 + lax.rem(i + (reps - 1) // 2, reps - 1))
        dispatch = fill(d)
        out_rows[d] = dot(dispatch[:cap], hidden[...]).astype(BF16)
        row_copy(d).start()
        out_ids[d] = dot(inner, dispatch, NT)
        id_copy(d).start()
        return c

    lax.fori_loop(0, reps - 1, send_rows, 0)

    half = tps // 2
    gather_copy(hidden, sibling, me_t, 0).start()
    for k in range(1, half):
        gather_copy(hidden, tp_at(2 * k), me_t, k).start()

    dispatch = fill(me_r)
    in_rows[me_r] = dot(dispatch[:cap], hidden[...]).astype(BF16)
    in_ids[me_r] = dot(inner, dispatch, NT)

    diagonal = iota((rows, rows), 0) == iota((rows, rows), 1)
    length_col = jnp.sum(jnp.where(diagonal, lengths[...].astype(F32), 0.0), axis=1, keepdims=True)
    length_v[...] = jnp.broadcast_to(length_col, (rows, HD))

    inverse = 1.0 / HD**0.5
    loads[0].wait()
    loads[1].wait()
    loads[2].wait()

    def attend(b, c):
        at = pl.ds(pl.multiple_of(b * ROW_BLOCK, ROW_BLOCK), ROW_BLOCK)
        column = iota((ROW_BLOCK, span), 1).astype(F32)
        low = (iota((ROW_BLOCK, span), 0) * positions).astype(F32)
        high = low + length_v[at, 0:1]
        bias = jnp.where((column >= low) & (column < high), 0.0, MASKED)
        for g in range(kv_local):
            feats = slice(g * HD, (g + 1) * HD)
            heads = [slice((g * group + j) * HD, (g * group + j + 1) * HD) for j in range(group)]
            query = jnp.concatenate([q_v[at, h] for h in heads], axis=0)
            keys = k_v[at, :, feats].reshape(span, HD)
            values = v_v[at, :, feats].reshape(span, HD)
            scores = dot(query, keys, NT).reshape(group, ROW_BLOCK, span) * inverse + bias[None]
            own = (
                jnp.sum(
                    query.astype(F32).reshape(group, ROW_BLOCK, HD) * fresh[at, feats].astype(F32)[None],
                    axis=-1, keepdims=True,
                )
                * inverse
            )
            top = jnp.maximum(jnp.max(scores, axis=-1, keepdims=True), own)
            expo = jnp.exp(scores - top)
            own_expo = jnp.exp(own - top)
            scale = 1.0 / (jnp.sum(expo, axis=-1, keepdims=True) + own_expo)
            weights = (expo * scale).astype(BF16).reshape(group * ROW_BLOCK, span)
            own_weight = jnp.broadcast_to(
                (own_expo * scale).astype(BF16).astype(F32), (group, ROW_BLOCK, HD)
            )
            mixed = dot(weights, values)
            for j, h in enumerate(heads):
                mixed_v[at, h] = mixed[j * ROW_BLOCK:(j + 1) * ROW_BLOCK]
                own_v[at, h] = own_weight[j]
        return c

    blocks = rows // ROW_BLOCK
    early = blocks // 2
    lax.fori_loop(0, early, attend, 0)
    for k in range(1, half):
        q = tp_at(2 * k)
        gather_copy(hidden, q, q, 0).wait_recv()
        gather_copy(shards.at[q], sibling, q, half + k).start()
    lax.fori_loop(early, blocks, attend, 0)

    loads[4].wait()
    base = dot(hidden[...], w_v[me_t])
    for k in range(1, half):
        q = tp_at(2 * k)
        base = base + dot(shards[q], w_v[q])
    for k in range(half):
        q = lax.rem(sibling + 2 * k, tps)
        gather_copy(hidden, q, q, 0).wait_recv()
        base = base + dot(shards[q], w_v[q])

    loads[3].wait()
    loads[5].wait()

    def part_copy(k, s):
        return pltpu.make_async_remote_copy(
            src_ref=part.at[s], dst_ref=parts.at[me_t, s], send_sem=part_send.at[k, s],
            recv_sem=part_recv.at[me_t, s], device_id={"tp": tp_at(k)}, device_id_type=pl.DeviceIdType.MESH,
        )

    def part_arrival(k, s):
        q = tp_at(k)
        return pltpu.make_async_remote_copy(
            src_ref=part.at[s], dst_ref=parts.at[q, s], send_sem=part_send.at[k, s],
            recv_sem=part_recv.at[q, s], device_id={"tp": q}, device_id_type=pl.DeviceIdType.MESH,
        )

    def delta_copy(s):
        return pltpu.make_async_remote_copy(
            src_ref=out_delta.at[s], dst_ref=in_delta.at[me_r], send_sem=delta_send.at[s],
            recv_sem=delta_recv.at[me_r], device_id={"rep": s}, device_id_type=pl.DeviceIdType.MESH,
        )

    def delta_arrival(s):
        return pltpu.make_async_remote_copy(
            src_ref=out_delta.at[s], dst_ref=in_delta.at[s], send_sem=delta_send.at[s],
            recv_sem=delta_recv.at[s], device_id={"rep": s}, device_id_type=pl.DeviceIdType.MESH,
        )

    def chosen(s):
        return iota((stored, rank, cap), 0).astype(F32) == in_ids[s][0:1, :cap].reshape(1, 1, cap)

    def shrink(s):
        full = dot(down_v[...], in_rows[s], NT).reshape(stored, rank, cap)
        part[s] = jnp.sum(jnp.where(chosen(s), full, 0.0), axis=0)
        for k in range(1, tps):
            part_copy(k, s).start()

    def expand(s):
        total = part[s]
        for k in range(1, tps):
            part_arrival(k, s).wait_recv()
            total = total + parts[tp_at(k), s]
        total = total.astype(BF16).astype(F32)
        spread = jnp.where(chosen(s), total[None], 0.0).reshape(stored * rank, cap).astype(BF16)
        return (ADAPTER_SCALE * dot(spread, up_v[...], TN)).astype(BF16)

    def step(i, c):
        s = rep_at(i)
        row_arrival(s).wait_recv()
        id_arrival(s).wait_recv()
        shrink(s)

        @pl.when(i == 1)
        def _():
            in_delta[me_r] = expand(me_r)

        @pl.when(i > 1)
        def _():
            back = rep_at(i - 1)
            out_delta[back] = expand(back)
            delta_copy(back).start()

        return c

    shrink(me_r)
    lax.fori_loop(1, reps, step, 0)
    last = rep_at(reps - 1)
    out_delta[last] = expand(last)
    delta_copy(last).start()

    value_v[...] = base + dot(slots[me_r][:cap], in_delta[me_r], TN)

    def collect(i, c):
        s = rep_at(reps - i)
        delta_arrival(s).wait_recv()
        value_v[...] += dot(slots[s][:cap], in_delta[s], TN)
        return c

    lax.fori_loop(1, reps, collect, 0)

    value = value_v[...].astype(BF16)
    value_out[...] = value
    fresh_value = value.astype(F32)
    for g in range(kv_local):
        for j in range(group):
            h = slice((g * group + j) * HD, (g * group + j + 1) * HD)
            attended_out[:, h] = (mixed_v[:, h] + own_v[:, h] * fresh_value[:, g * HD:(g + 1) * HD]).astype(BF16)

    gather_copy(hidden, sibling, me_t, 0).wait_send()
    for k in range(1, half):
        gather_copy(hidden, sibling, me_t, k).wait_send()
        gather_copy(hidden, sibling, me_t, half + k).wait_send()

    def drain(i, c):
        d = rep_at(i)
        row_copy(d).wait_send()
        id_copy(d).wait_send()
        delta_copy(d).wait_send()
        return c

    lax.fori_loop(1, reps, drain, 0)

    def drain_parts(s, c):
        for k in range(1, tps):
            part_copy(k, s).wait_send()
        return c

    lax.fori_loop(0, reps, drain_parts, 0)


def shards_fn(
    hidden, queries, fresh_token_keys, cached_key_rows, cached_value_rows, lengths, row_adapter_index,
    adapter_table_place, value_projection_matrix, adapter_down_factor, adapter_up_factor,
):
    reps, tps = lax.axis_size("rep"), lax.axis_size("tp")
    rows, width = hidden.shape
    stored, rank, _ = adapter_down_factor.shape
    out_width = adapter_up_factor.shape[2]
    cap = max(2, (2 * rows + reps - 1) // reps)
    dma = pltpu.SemaphoreType.DMA
    vmem = pltpu.VMEM
    w = value_projection_matrix.reshape(tps, width, out_width)
    scratch = [
        vmem(queries.shape, BF16), vmem(cached_key_rows.shape, BF16), vmem(cached_value_rows.shape, BF16),
        vmem(w.shape, BF16), vmem((stored * rank, width), BF16), vmem((stored * rank, out_width), BF16), dma((6,)),
        vmem((tps, rows, width), BF16),
        vmem((reps, cap, width), BF16), vmem((reps, cap, width), BF16),
        vmem((reps, 8, rows), F32), vmem((reps, 8, rows), F32),
        vmem((reps, rows, rows), BF16),
        vmem((reps, rank, cap), F32), vmem((tps, reps, rank, cap), F32),
        vmem((reps, cap, out_width), BF16), vmem((reps, cap, out_width), BF16),
        vmem(queries.shape, F32), vmem(queries.shape, F32), vmem((rows, HD), F32), vmem((rows, out_width), F32),
        vmem((8, 128), F32),
        dma((tps,)), dma((tps,)), dma((reps,)), dma((reps,)), dma((reps,)), dma((reps,)),
        dma((tps, reps)), dma((tps, reps)), dma((reps,)), dma((reps,)),
    ]
    vm, anywhere = pl.BlockSpec(memory_space=pltpu.VMEM), pl.BlockSpec(memory_space=pl.ANY)
    return pl.pallas_call(
        functools.partial(kernel, reps, tps, cap, stored, rank),
        out_shape=(
            jax.ShapeDtypeStruct((rows, out_width), BF16),
            jax.ShapeDtypeStruct(queries.shape, BF16),
        ),
        in_specs=[vm] * 5 + [anywhere] * 6,
        out_specs=(vm, vm),
        scratch_shapes=scratch,
        compiler_params=pltpu.CompilerParams(
            collective_id=0, has_side_effects=True, vmem_limit_bytes=48 * 1024 * 1024
        ),
    )(
        hidden, fresh_token_keys, lengths.reshape(1, rows), row_adapter_index.reshape(1, rows),
        adapter_table_place.reshape(1, -1), queries, cached_key_rows, cached_value_rows, w,
        adapter_down_factor.reshape(stored * rank, width), adapter_up_factor.reshape(stored * rank, out_width),
    )


def solution(mesh):
    return jax.shard_map(
        shards_fn,
        mesh=mesh,
        in_specs=(
            P(("groups", "rep"), "tp"),
            P(("groups", "rep"), "tp"),
            P(("groups", "rep"), "tp"),
            P(("groups", "rep"), None, "tp"),
            P(("groups", "rep"), None, "tp"),
            P(("groups", "rep")),
            P(("groups", "rep")),
            P("groups"),
            P(None, "tp"),
            P(("groups", "rep"), None, "tp"),
            P(("groups", "rep"), None, "tp"),
        ),
        out_specs=(P(("groups", "rep"), "tp"), P(("groups", "rep"), "tp")),
        check_vma=False,
    )
```

```python
import functools

import jax
import jax.numpy as jnp
from jax import lax
from jax.experimental import pallas as pl
from jax.experimental.pallas import tpu as pltpu
from jax.sharding import PartitionSpec as P

HD = 128
ROW_BLOCK = 16
ADAPTER_SCALE = 2.0
MASKED = -1e30
F32, BF16 = jnp.float32, jnp.bfloat16
NT = (((1,), (1,)), ((), ()))
TN = (((0,), (0,)), ((), ()))
NN = (((1,), (0,)), ((), ()))


def dot(a, b, dims=NN):
    return lax.dot_general(a, b, dims, preferred_element_type=F32)


def iota(shape, dim):
    return lax.broadcasted_iota(jnp.int32, shape, dim)


def kernel(
    reps, tps, cap, stored, rank,
    hidden_hbm, fresh_hbm, lengths_hbm, index_hbm, places_hbm, q_hbm, k_hbm, v_hbm, w_hbm, down_hbm, up_hbm,
    value_out, attended_out,
    hidden, fresh, lengths, index, places,
    q_v, k_v, v_v, w_v, down_v, up_v, local_sem,
    shards, out_rows, in_rows, out_ids, in_ids, slots, part, parts, out_delta, in_delta,
    mixed_v, own_v, length_v, value_v,
    gather_send, gather_recv, row_send, row_recv, id_send, id_recv,
    part_send, part_recv, delta_send, delta_recv,
):
    me_r, me_t = lax.axis_index("rep"), lax.axis_index("tp")
    rows, kv_local = hidden.shape[0], fresh.shape[1] // HD
    group = q_v.shape[1] // fresh.shape[1]
    positions = k_v.shape[1]
    span = ROW_BLOCK * positions

    def rep_at(k):
        return lax.rem(me_r + k, reps)

    rep_sibling = me_r + 1 - 2 * lax.rem(me_r, 2)

    def rep_near(i):
        odd = lax.rem(i, 2)
        return lax.rem(odd * rep_sibling + (1 - odd) * me_r + 2 * (i // 2), reps)

    def tp_at(k):
        return lax.rem(me_t + k, tps)

    sibling = me_t + 1 - 2 * lax.rem(me_t, 2)

    loads = [
        pltpu.make_async_copy(src, dst, local_sem.at[n])
        for n, (src, dst) in enumerate(
            (
                (q_hbm, q_v), (k_hbm, k_v), (v_hbm, v_v), (down_hbm, down_v), (w_hbm, w_v), (up_hbm, up_v),
                (index_hbm, index), (places_hbm, places), (hidden_hbm, hidden), (lengths_hbm, lengths), (fresh_hbm, fresh),
            )
        )
    ]
    for n in (6, 7, 8, 9, 10, 0, 1, 2, 3, 5, 4):
        loads[n].start()

    barrier = pltpu.get_barrier_semaphore()

    def greet_rep(k, c):
        pl.semaphore_signal(barrier, inc=1, device_id={"rep": rep_at(k)}, device_id_type=pl.DeviceIdType.MESH)
        return c

    def greet_tp(k, c):
        pl.semaphore_signal(barrier, inc=1, device_id={"tp": tp_at(k)}, device_id_type=pl.DeviceIdType.MESH)
        return c

    lax.fori_loop(1, reps, greet_rep, 0)
    lax.fori_loop(1, tps, greet_tp, 0)

    loads[6].wait()
    loads[7].wait()
    adapters = places.shape[1]
    place = places[...].astype(F32)
    owner_tab = jnp.floor((place + 0.5) / stored)
    inner_tab = place - owner_tab * stored
    hot = (iota((adapters, rows), 0) == index[...]).astype(F32).astype(BF16)
    owner = dot(jnp.broadcast_to(owner_tab, (8, adapters)).astype(BF16), hot)
    inner = dot(jnp.broadcast_to(inner_tab, (8, adapters)).astype(BF16), hot).astype(BF16)
    rep_pad = max(8, reps)
    owner_row = owner[0:1, :]
    owner_hot = (iota((rep_pad, rows), 0).astype(F32) == owner_row).astype(F32)
    earlier = (iota((rows, rows), 0) < iota((rows, rows), 1)).astype(F32).astype(BF16)
    before = dot(owner_hot.astype(BF16), earlier)
    position = jnp.sum(before * owner_hot, axis=0, keepdims=True)
    slot_iota = iota((rows, rows), 0).astype(F32)

    def gather_copy(src, to, q, n):
        return pltpu.make_async_remote_copy(
            src_ref=src, dst_ref=shards.at[q], send_sem=gather_send.at[n], recv_sem=gather_recv.at[q],
            device_id={"tp": to}, device_id_type=pl.DeviceIdType.MESH,
        )

    def row_copy(d):
        return pltpu.make_async_remote_copy(
            src_ref=out_rows.at[d], dst_ref=in_rows.at[me_r], send_sem=row_send.at[d], recv_sem=row_recv.at[me_r],
            device_id={"rep": d}, device_id_type=pl.DeviceIdType.MESH,
        )

    def id_copy(d):
        return pltpu.make_async_remote_copy(
            src_ref=out_ids.at[d], dst_ref=in_ids.at[me_r], send_sem=id_send.at[d], recv_sem=id_recv.at[me_r],
            device_id={"rep": d}, device_id_type=pl.DeviceIdType.MESH,
        )

    def row_arrival(s):
        return pltpu.make_async_remote_copy(
            src_ref=out_rows.at[s], dst_ref=in_rows.at[s], send_sem=row_send.at[s], recv_sem=row_recv.at[s],
            device_id={"rep": s}, device_id_type=pl.DeviceIdType.MESH,
        )

    def id_arrival(s):
        return pltpu.make_async_remote_copy(
            src_ref=out_ids.at[s], dst_ref=in_ids.at[s], send_sem=id_send.at[s], recv_sem=id_recv.at[s],
            device_id={"rep": s}, device_id_type=pl.DeviceIdType.MESH,
        )

    def fill(d):
        member = jnp.where(owner_row == d.astype(F32), position, -1.0)
        dispatch = (slot_iota == member).astype(F32).astype(BF16)
        slots[d] = dispatch
        return dispatch

    loads[8].wait()
    pl.semaphore_wait(barrier, reps - 1 + tps - 1)

    def send_rows(i, c):
        d = rep_near(reps - 1 - i)
        dispatch = fill(d)
        out_rows[d] = dot(dispatch[:cap], hidden[...]).astype(BF16)
        row_copy(d).start()
        out_ids[d] = dot(inner, dispatch, NT)
        id_copy(d).start()
        return c

    lax.fori_loop(0, reps - 1, send_rows, 0)

    half = tps // 2
    gather_copy(hidden, sibling, me_t, 0).start()
    for k in range(1, half):
        gather_copy(hidden, tp_at(2 * k), me_t, k).start()

    dispatch = fill(me_r)
    in_rows[me_r] = dot(dispatch[:cap], hidden[...]).astype(BF16)
    in_ids[me_r] = dot(inner, dispatch, NT)

    loads[9].wait()
    diagonal = iota((rows, rows), 0) == iota((rows, rows), 1)
    length_col = jnp.sum(jnp.where(diagonal, lengths[...].astype(F32), 0.0), axis=1, keepdims=True)
    length_v[...] = jnp.broadcast_to(length_col, (rows, HD))

    inverse = 1.0 / HD**0.5
    loads[0].wait()
    loads[1].wait()
    loads[2].wait()
    loads[10].wait()

    def attend(b, c):
        at = pl.ds(pl.multiple_of(b * ROW_BLOCK, ROW_BLOCK), ROW_BLOCK)
        column = iota((ROW_BLOCK, span), 1).astype(F32)
        low = (iota((ROW_BLOCK, span), 0) * positions).astype(F32)
        high = low + length_v[at, 0:1]
        bias = jnp.where((column >= low) & (column < high), 0.0, MASKED)
        for g in range(kv_local):
            feats = slice(g * HD, (g + 1) * HD)
            heads = [slice((g * group + j) * HD, (g * group + j + 1) * HD) for j in range(group)]
            query = jnp.concatenate([q_v[at, h] for h in heads], axis=0)
            keys = k_v[at, :, feats].reshape(span, HD)
            values = v_v[at, :, feats].reshape(span, HD)
            scores = dot(query, keys, NT).reshape(group, ROW_BLOCK, span) * inverse + bias[None]
            own = (
                jnp.sum(
                    query.astype(F32).reshape(group, ROW_BLOCK, HD) * fresh[at, feats].astype(F32)[None],
                    axis=-1, keepdims=True,
                )
                * inverse
            )
            top = jnp.maximum(jnp.max(scores, axis=-1, keepdims=True), own)
            expo = jnp.exp(scores - top)
            own_expo = jnp.exp(own - top)
            scale = 1.0 / (jnp.sum(expo, axis=-1, keepdims=True) + own_expo)
            weights = (expo * scale).astype(BF16).reshape(group * ROW_BLOCK, span)
            own_weight = jnp.broadcast_to(
                (own_expo * scale).astype(BF16).astype(F32), (group, ROW_BLOCK, HD)
            )
            mixed = dot(weights, values)
            for j, h in enumerate(heads):
                mixed_v[at, h] = mixed[j * ROW_BLOCK:(j + 1) * ROW_BLOCK]
                own_v[at, h] = own_weight[j]
        return c

    blocks = rows // ROW_BLOCK
    early = blocks // 2
    lax.fori_loop(0, early, attend, 0)
    for k in range(1, half):
        q = tp_at(2 * k)
        gather_copy(hidden, q, q, 0).wait_recv()
        gather_copy(shards.at[q], sibling, q, half + k).start()
    lax.fori_loop(early, blocks, attend, 0)

    loads[4].wait()
    base = dot(hidden[...], w_v[me_t])
    for k in range(1, half):
        q = tp_at(2 * k)
        base = base + dot(shards[q], w_v[q])
    for k in range(half):
        q = lax.rem(sibling + 2 * k, tps)
        gather_copy(hidden, q, q, 0).wait_recv()
        base = base + dot(shards[q], w_v[q])

    loads[3].wait()
    loads[5].wait()

    def part_copy(k, s):
        return pltpu.make_async_remote_copy(
            src_ref=part.at[s], dst_ref=parts.at[me_t, s], send_sem=part_send.at[k, s],
            recv_sem=part_recv.at[me_t, s], device_id={"tp": tp_at(k)}, device_id_type=pl.DeviceIdType.MESH,
        )

    def part_arrival(k, s):
        q = tp_at(k)
        return pltpu.make_async_remote_copy(
            src_ref=part.at[s], dst_ref=parts.at[q, s], send_sem=part_send.at[k, s],
            recv_sem=part_recv.at[q, s], device_id={"tp": q}, device_id_type=pl.DeviceIdType.MESH,
        )

    def delta_copy(s):
        return pltpu.make_async_remote_copy(
            src_ref=out_delta.at[s], dst_ref=in_delta.at[me_r], send_sem=delta_send.at[s],
            recv_sem=delta_recv.at[me_r], device_id={"rep": s}, device_id_type=pl.DeviceIdType.MESH,
        )

    def delta_arrival(s):
        return pltpu.make_async_remote_copy(
            src_ref=out_delta.at[s], dst_ref=in_delta.at[s], send_sem=delta_send.at[s],
            recv_sem=delta_recv.at[s], device_id={"rep": s}, device_id_type=pl.DeviceIdType.MESH,
        )

    def chosen(s):
        return iota((stored, rank, cap), 0).astype(F32) == in_ids[s][0:1, :cap].reshape(1, 1, cap)

    def shrink(s):
        full = dot(down_v[...], in_rows[s], NT).reshape(stored, rank, cap)
        part[s] = jnp.sum(jnp.where(chosen(s), full, 0.0), axis=0)
        for k in range(1, tps):
            part_copy(k, s).start()

    def expand(s):
        total = part[s]
        for k in range(1, tps):
            part_arrival(k, s).wait_recv()
            total = total + parts[tp_at(k), s]
        total = total.astype(BF16).astype(F32)
        spread = jnp.where(chosen(s), total[None], 0.0).reshape(stored * rank, cap).astype(BF16)
        return (ADAPTER_SCALE * dot(spread, up_v[...], TN)).astype(BF16)

    def step(i, c):
        s = rep_near(i)
        row_arrival(s).wait_recv()
        id_arrival(s).wait_recv()
        shrink(s)

        @pl.when(i == 1)
        def _():
            in_delta[me_r] = expand(me_r)

        @pl.when(i > 1)
        def _():
            back = rep_near(i - 1)
            out_delta[back] = expand(back)
            delta_copy(back).start()

        return c

    shrink(me_r)
    lax.fori_loop(1, reps, step, 0)
    last = rep_near(reps - 1)
    out_delta[last] = expand(last)
    delta_copy(last).start()

    value_v[...] = base + dot(slots[me_r][:cap], in_delta[me_r], TN)

    def collect(i, c):
        s = rep_near(i)
        delta_arrival(s).wait_recv()
        value_v[...] += dot(slots[s][:cap], in_delta[s], TN)
        return c

    lax.fori_loop(1, reps, collect, 0)

    value = value_v[...].astype(BF16)
    value_out[...] = value
    fresh_value = value.astype(F32)
    for g in range(kv_local):
        for j in range(group):
            h = slice((g * group + j) * HD, (g * group + j + 1) * HD)
            attended_out[:, h] = (mixed_v[:, h] + own_v[:, h] * fresh_value[:, g * HD:(g + 1) * HD]).astype(BF16)

    gather_copy(hidden, sibling, me_t, 0).wait_send()
    for k in range(1, half):
        gather_copy(hidden, sibling, me_t, k).wait_send()
        gather_copy(hidden, sibling, me_t, half + k).wait_send()

    def drain(i, c):
        d = rep_at(i)
        row_copy(d).wait_send()
        id_copy(d).wait_send()
        delta_copy(d).wait_send()
        return c

    lax.fori_loop(1, reps, drain, 0)

    def drain_parts(s, c):
        for k in range(1, tps):
            part_copy(k, s).wait_send()
        return c

    lax.fori_loop(0, reps, drain_parts, 0)


def shards_fn(
    hidden, queries, fresh_token_keys, cached_key_rows, cached_value_rows, lengths, row_adapter_index,
    adapter_table_place, value_projection_matrix, adapter_down_factor, adapter_up_factor,
):
    reps, tps = lax.axis_size("rep"), lax.axis_size("tp")
    rows, width = hidden.shape
    stored, rank, _ = adapter_down_factor.shape
    out_width = adapter_up_factor.shape[2]
    cap = max(2, (2 * rows + reps - 1) // reps)
    dma = pltpu.SemaphoreType.DMA
    vmem = pltpu.VMEM
    w = value_projection_matrix.reshape(tps, width, out_width)
    adapters = adapter_table_place.shape[0]
    scratch = [
        vmem(hidden.shape, BF16), vmem(fresh_token_keys.shape, BF16),
        vmem((1, rows), jnp.int32), vmem((1, rows), jnp.int32), vmem((1, adapters), jnp.int32),
        vmem(queries.shape, BF16), vmem(cached_key_rows.shape, BF16), vmem(cached_value_rows.shape, BF16),
        vmem(w.shape, BF16), vmem((stored * rank, width), BF16), vmem((stored * rank, out_width), BF16), dma((11,)),
        vmem((tps, rows, width), BF16),
        vmem((reps, cap, width), BF16), vmem((reps, cap, width), BF16),
        vmem((reps, 8, rows), F32), vmem((reps, 8, rows), F32),
        vmem((reps, rows, rows), BF16),
        vmem((reps, rank, cap), F32), vmem((tps, reps, rank, cap), F32),
        vmem((reps, cap, out_width), BF16), vmem((reps, cap, out_width), BF16),
        vmem(queries.shape, F32), vmem(queries.shape, F32), vmem((rows, HD), F32), vmem((rows, out_width), F32),
        dma((tps,)), dma((tps,)), dma((reps,)), dma((reps,)), dma((reps,)), dma((reps,)),
        dma((tps, reps)), dma((tps, reps)), dma((reps,)), dma((reps,)),
    ]
    vm, anywhere = pl.BlockSpec(memory_space=pltpu.VMEM), pl.BlockSpec(memory_space=pl.ANY)
    return pl.pallas_call(
        functools.partial(kernel, reps, tps, cap, stored, rank),
        out_shape=(
            jax.ShapeDtypeStruct((rows, out_width), BF16),
            jax.ShapeDtypeStruct(queries.shape, BF16),
        ),
        in_specs=[anywhere] * 11,
        out_specs=(vm, vm),
        scratch_shapes=scratch,
        compiler_params=pltpu.CompilerParams(
            collective_id=0, has_side_effects=True, vmem_limit_bytes=60 * 1024 * 1024
        ),
    )(
        hidden, fresh_token_keys, lengths.reshape(1, rows), row_adapter_index.reshape(1, rows),
        adapter_table_place.reshape(1, -1), queries, cached_key_rows, cached_value_rows, w,
        adapter_down_factor.reshape(stored * rank, width), adapter_up_factor.reshape(stored * rank, out_width),
    )


def solution(mesh):
    return jax.shard_map(
        shards_fn,
        mesh=mesh,
        in_specs=(
            P(("groups", "rep"), "tp"),
            P(("groups", "rep"), "tp"),
            P(("groups", "rep"), "tp"),
            P(("groups", "rep"), None, "tp"),
            P(("groups", "rep"), None, "tp"),
            P(("groups", "rep")),
            P(("groups", "rep")),
            P("groups"),
            P(None, "tp"),
            P(("groups", "rep"), None, "tp"),
            P(("groups", "rep"), None, "tp"),
        ),
        out_specs=(P(("groups", "rep"), "tp"), P(("groups", "rep"), "tp")),
        check_vma=False,
    )
```

```python
import functools

import jax
import jax.numpy as jnp
from jax import lax
from jax.experimental import pallas as pl
from jax.experimental.pallas import tpu as pltpu
from jax.sharding import PartitionSpec as P

HD = 128
ROW_BLOCK = 16
ADAPTER_SCALE = 2.0
MASKED = -1e30
F32, BF16 = jnp.float32, jnp.bfloat16
NT = (((1,), (1,)), ((), ()))
TN = (((0,), (0,)), ((), ()))
NN = (((1,), (0,)), ((), ()))


def dot(a, b, dims=NN):
    return lax.dot_general(a, b, dims, preferred_element_type=F32)


def iota(shape, dim):
    return lax.broadcasted_iota(jnp.int32, shape, dim)


def kernel(
    reps, tps, cap, stored, rank,
    hidden_hbm, fresh_hbm, lengths_hbm, index_hbm, places_hbm, q_hbm, k_hbm, v_hbm, w_hbm, down_hbm, up_hbm,
    value_out, attended_out,
    hidden, fresh, lengths, index, places,
    q_v, k_v, v_v, w_v, down_v, up_v, local_sem,
    shards, out_rows, in_rows, out_ids, in_ids, slots, part, parts, out_delta, in_delta,
    mixed_v, own_v, length_v, value_v, value_b, attended_v, store_sem,
    gather_send, gather_recv, row_send, row_recv, id_send, id_recv,
    part_send, part_recv, delta_send, delta_recv,
):
    me_r, me_t = lax.axis_index("rep"), lax.axis_index("tp")
    rows, kv_local = hidden.shape[0], fresh.shape[1] // HD
    group = q_v.shape[1] // fresh.shape[1]
    positions = k_v.shape[1]
    span = ROW_BLOCK * positions

    def rep_at(k):
        return lax.rem(me_r + k, reps)

    rep_sibling = me_r + 1 - 2 * lax.rem(me_r, 2)

    def rep_near(i):
        odd = lax.rem(i, 2)
        return lax.rem(odd * rep_sibling + (1 - odd) * me_r + 2 * (i // 2), reps)

    def tp_at(k):
        return lax.rem(me_t + k, tps)

    sibling = me_t + 1 - 2 * lax.rem(me_t, 2)

    loads = [
        pltpu.make_async_copy(src, dst, local_sem.at[n])
        for n, (src, dst) in enumerate(
            (
                (q_hbm, q_v), (k_hbm, k_v), (v_hbm, v_v), (down_hbm, down_v), (w_hbm, w_v), (up_hbm, up_v),
                (index_hbm, index), (places_hbm, places), (hidden_hbm, hidden), (lengths_hbm, lengths), (fresh_hbm, fresh),
            )
        )
    ]
    for n in (6, 7, 8, 9, 10, 0, 1, 2, 3, 5, 4):
        loads[n].start()

    barrier = pltpu.get_barrier_semaphore()

    def greet_rep(k, c):
        pl.semaphore_signal(barrier, inc=1, device_id={"rep": rep_at(k)}, device_id_type=pl.DeviceIdType.MESH)
        return c

    def greet_tp(k, c):
        pl.semaphore_signal(barrier, inc=1, device_id={"tp": tp_at(k)}, device_id_type=pl.DeviceIdType.MESH)
        return c

    lax.fori_loop(1, reps, greet_rep, 0)
    lax.fori_loop(1, tps, greet_tp, 0)

    loads[6].wait()
    loads[7].wait()
    adapters = places.shape[1]
    place = places[...].astype(F32)
    owner_tab = jnp.floor((place + 0.5) / stored)
    inner_tab = place - owner_tab * stored
    hot = (iota((adapters, rows), 0) == index[...]).astype(F32).astype(BF16)
    owner = dot(jnp.broadcast_to(owner_tab, (8, adapters)).astype(BF16), hot)
    inner = dot(jnp.broadcast_to(inner_tab, (8, adapters)).astype(BF16), hot).astype(BF16)
    rep_pad = max(8, reps)
    owner_row = owner[0:1, :]
    owner_hot = (iota((rep_pad, rows), 0).astype(F32) == owner_row).astype(F32)
    earlier = (iota((rows, rows), 0) < iota((rows, rows), 1)).astype(F32).astype(BF16)
    before = dot(owner_hot.astype(BF16), earlier)
    position = jnp.sum(before * owner_hot, axis=0, keepdims=True)
    slot_iota = iota((rows, rows), 0).astype(F32)

    def gather_copy(src, to, q, n):
        return pltpu.make_async_remote_copy(
            src_ref=src, dst_ref=shards.at[q], send_sem=gather_send.at[n], recv_sem=gather_recv.at[q],
            device_id={"tp": to}, device_id_type=pl.DeviceIdType.MESH,
        )

    def row_copy(d):
        return pltpu.make_async_remote_copy(
            src_ref=out_rows.at[d], dst_ref=in_rows.at[me_r], send_sem=row_send.at[d], recv_sem=row_recv.at[me_r],
            device_id={"rep": d}, device_id_type=pl.DeviceIdType.MESH,
        )

    def id_copy(d):
        return pltpu.make_async_remote_copy(
            src_ref=out_ids.at[d], dst_ref=in_ids.at[me_r], send_sem=id_send.at[d], recv_sem=id_recv.at[me_r],
            device_id={"rep": d}, device_id_type=pl.DeviceIdType.MESH,
        )

    def row_arrival(s):
        return pltpu.make_async_remote_copy(
            src_ref=out_rows.at[s], dst_ref=in_rows.at[s], send_sem=row_send.at[s], recv_sem=row_recv.at[s],
            device_id={"rep": s}, device_id_type=pl.DeviceIdType.MESH,
        )

    def id_arrival(s):
        return pltpu.make_async_remote_copy(
            src_ref=out_ids.at[s], dst_ref=in_ids.at[s], send_sem=id_send.at[s], recv_sem=id_recv.at[s],
            device_id={"rep": s}, device_id_type=pl.DeviceIdType.MESH,
        )

    def fill(d):
        member = jnp.where(owner_row == d.astype(F32), position, -1.0)
        dispatch = (slot_iota == member).astype(F32).astype(BF16)
        slots[d] = dispatch
        return dispatch

    loads[8].wait()
    pl.semaphore_wait(barrier, reps - 1 + tps - 1)

    def send_rows(i, c):
        d = rep_near(1 + i)
        dispatch = fill(d)
        out_rows[d] = dot(dispatch[:cap], hidden[...]).astype(BF16)
        row_copy(d).start()
        out_ids[d] = dot(inner, dispatch, NT)
        id_copy(d).start()
        return c

    lax.fori_loop(0, reps - 1, send_rows, 0)

    half = tps // 2
    gather_copy(hidden, sibling, me_t, 0).start()
    for k in range(1, half):
        gather_copy(hidden, tp_at(2 * k), me_t, k).start()

    dispatch = fill(me_r)
    in_rows[me_r] = dot(dispatch[:cap], hidden[...]).astype(BF16)
    in_ids[me_r] = dot(inner, dispatch, NT)

    loads[9].wait()
    diagonal = iota((rows, rows), 0) == iota((rows, rows), 1)
    length_col = jnp.sum(jnp.where(diagonal, lengths[...].astype(F32), 0.0), axis=1, keepdims=True)
    length_v[...] = jnp.broadcast_to(length_col, (rows, HD))

    inverse = 1.0 / HD**0.5
    loads[0].wait()
    loads[1].wait()
    loads[2].wait()
    loads[10].wait()

    def attend(b, c):
        at = pl.ds(pl.multiple_of(b * ROW_BLOCK, ROW_BLOCK), ROW_BLOCK)
        column = iota((ROW_BLOCK, span), 1).astype(F32)
        low = (iota((ROW_BLOCK, span), 0) * positions).astype(F32)
        high = low + length_v[at, 0:1]
        bias = jnp.where((column >= low) & (column < high), 0.0, MASKED)
        for g in range(kv_local):
            feats = slice(g * HD, (g + 1) * HD)
            heads = [slice((g * group + j) * HD, (g * group + j + 1) * HD) for j in range(group)]
            query = jnp.concatenate([q_v[at, h] for h in heads], axis=0)
            keys = k_v[at, :, feats].reshape(span, HD)
            values = v_v[at, :, feats].reshape(span, HD)
            scores = dot(query, keys, NT).reshape(group, ROW_BLOCK, span) * inverse + bias[None]
            own = (
                jnp.sum(
                    query.astype(F32).reshape(group, ROW_BLOCK, HD) * fresh[at, feats].astype(F32)[None],
                    axis=-1, keepdims=True,
                )
                * inverse
            )
            top = jnp.maximum(jnp.max(scores, axis=-1, keepdims=True), own)
            expo = jnp.exp(scores - top)
            own_expo = jnp.exp(own - top)
            scale = 1.0 / (jnp.sum(expo, axis=-1, keepdims=True) + own_expo)
            weights = (expo * scale).astype(BF16).reshape(group * ROW_BLOCK, span)
            own_weight = jnp.broadcast_to(
                (own_expo * scale).astype(BF16).astype(F32), (group, ROW_BLOCK, HD)
            )
            mixed = dot(weights, values)
            for j, h in enumerate(heads):
                mixed_v[at, h] = mixed[j * ROW_BLOCK:(j + 1) * ROW_BLOCK]
                own_v[at, h] = own_weight[j]
        return c


    def part_copy(k, s):
        return pltpu.make_async_remote_copy(
            src_ref=part.at[s], dst_ref=parts.at[me_t, s], send_sem=part_send.at[k, s],
            recv_sem=part_recv.at[me_t, s], device_id={"tp": tp_at(k)}, device_id_type=pl.DeviceIdType.MESH,
        )

    def part_arrival(k, s):
        q = tp_at(k)
        return pltpu.make_async_remote_copy(
            src_ref=part.at[s], dst_ref=parts.at[q, s], send_sem=part_send.at[k, s],
            recv_sem=part_recv.at[q, s], device_id={"tp": q}, device_id_type=pl.DeviceIdType.MESH,
        )

    def delta_copy(s):
        return pltpu.make_async_remote_copy(
            src_ref=out_delta.at[s], dst_ref=in_delta.at[me_r], send_sem=delta_send.at[s],
            recv_sem=delta_recv.at[me_r], device_id={"rep": s}, device_id_type=pl.DeviceIdType.MESH,
        )

    def delta_arrival(s):
        return pltpu.make_async_remote_copy(
            src_ref=out_delta.at[s], dst_ref=in_delta.at[s], send_sem=delta_send.at[s],
            recv_sem=delta_recv.at[s], device_id={"rep": s}, device_id_type=pl.DeviceIdType.MESH,
        )

    def chosen(s):
        return iota((stored, rank, cap), 0).astype(F32) == in_ids[s][0:1, :cap].reshape(1, 1, cap)

    def shrink(s):
        full = dot(down_v[...], in_rows[s], NT).reshape(stored, rank, cap)
        part[s] = jnp.sum(jnp.where(chosen(s), full, 0.0), axis=0)
        for k in range(1, tps):
            part_copy(k, s).start()

    def expand(s):
        total = part[s]
        for k in range(1, tps):
            part_arrival(k, s).wait_recv()
            total = total + parts[tp_at(k), s]
        total = total.astype(BF16).astype(F32)
        spread = jnp.where(chosen(s), total[None], 0.0).reshape(stored * rank, cap).astype(BF16)
        return (ADAPTER_SCALE * dot(spread, up_v[...], TN)).astype(BF16)

    def forward():
        for k in range(1, half):
            q = tp_at(2 * k)
            gather_copy(hidden, q, q, 0).wait_recv()
            gather_copy(shards.at[q], sibling, q, half + k).start()
        loads[4].wait()
        value_v[...] = dot(hidden[...], w_v[me_t])
        in_delta[me_r] = expand(me_r)

    def finish_base():
        base = value_v[...]
        for k in range(1, half):
            q = tp_at(2 * k)
            base = base + dot(shards[q], w_v[q])
        for k in range(half):
            q = lax.rem(sibling + 2 * k, tps)
            gather_copy(hidden, q, q, 0).wait_recv()
            base = base + dot(shards[q], w_v[q])
        value_v[...] = base + dot(slots[me_r][:cap], in_delta[me_r], TN)

    def step(i, c):
        s = rep_near(i)
        row_arrival(s).wait_recv()
        id_arrival(s).wait_recv()
        shrink(s)
        pl.when(i == 1)(forward)
        pl.when(i == min(2, reps - 1))(finish_base)
        out_delta[s] = expand(s)
        delta_copy(s).start()
        return c

    blocks = rows // ROW_BLOCK
    early = blocks // 2
    lax.fori_loop(0, early, attend, 0)
    loads[3].wait()
    loads[5].wait()
    shrink(me_r)
    lax.fori_loop(early, blocks, attend, 0)
    lax.fori_loop(1, reps, step, 0)

    def collect(i, c):
        s = rep_near(i)
        delta_arrival(s).wait_recv()
        value_v[...] += dot(slots[s][:cap], in_delta[s], TN)
        return c

    lax.fori_loop(1, reps, collect, 0)

    value = value_v[...].astype(BF16)
    value_b[...] = value
    stores = [pltpu.make_async_copy(value_b, value_out, store_sem.at[0])]
    stores[0].start()
    fresh_value = value.astype(F32)
    for g in range(kv_local):
        for j in range(group):
            h = slice((g * group + j) * HD, (g * group + j + 1) * HD)
            attended_v[:, h] = (mixed_v[:, h] + own_v[:, h] * fresh_value[:, g * HD:(g + 1) * HD]).astype(BF16)
        part_cols = pl.ds(g * group * HD, group * HD)
        stores.append(
            pltpu.make_async_copy(attended_v.at[:, part_cols], attended_out.at[:, part_cols], store_sem.at[1 + g])
        )
        stores[-1].start()

    gather_copy(hidden, sibling, me_t, 0).wait_send()
    for k in range(1, half):
        gather_copy(hidden, sibling, me_t, k).wait_send()
        gather_copy(hidden, sibling, me_t, half + k).wait_send()

    def drain(i, c):
        d = rep_at(i)
        row_copy(d).wait_send()
        id_copy(d).wait_send()
        delta_copy(d).wait_send()
        return c

    lax.fori_loop(1, reps, drain, 0)

    def drain_parts(s, c):
        for k in range(1, tps):
            part_copy(k, s).wait_send()
        return c

    lax.fori_loop(0, reps, drain_parts, 0)
    for store in stores:
        store.wait()


def hand_over(value, attended, value_out, attended_out, sem):
    copies = [
        pltpu.make_async_copy(value, value_out, sem.at[0]),
        pltpu.make_async_copy(attended, attended_out, sem.at[1]),
    ]
    for copy in copies:
        copy.start()
    for copy in copies:
        copy.wait()


def shards_fn(
    hidden, queries, fresh_token_keys, cached_key_rows, cached_value_rows, lengths, row_adapter_index,
    adapter_table_place, value_projection_matrix, adapter_down_factor, adapter_up_factor,
):
    reps, tps = lax.axis_size("rep"), lax.axis_size("tp")
    rows, width = hidden.shape
    stored, rank, _ = adapter_down_factor.shape
    out_width = adapter_up_factor.shape[2]
    cap = max(2, (2 * rows + reps - 1) // reps)
    dma = pltpu.SemaphoreType.DMA
    vmem = pltpu.VMEM
    w = value_projection_matrix.reshape(tps, width, out_width)
    adapters = adapter_table_place.shape[0]
    scratch = [
        vmem(hidden.shape, BF16), vmem(fresh_token_keys.shape, BF16),
        vmem((1, rows), jnp.int32), vmem((1, rows), jnp.int32), vmem((1, adapters), jnp.int32),
        vmem(queries.shape, BF16), vmem(cached_key_rows.shape, BF16), vmem(cached_value_rows.shape, BF16),
        vmem(w.shape, BF16), vmem((stored * rank, width), BF16), vmem((stored * rank, out_width), BF16), dma((11,)),
        vmem((tps, rows, width), BF16),
        vmem((reps, cap, width), BF16), vmem((reps, cap, width), BF16),
        vmem((reps, 8, rows), F32), vmem((reps, 8, rows), F32),
        vmem((reps, rows, rows), BF16),
        vmem((reps, rank, cap), F32), vmem((tps, reps, rank, cap), F32),
        vmem((reps, cap, out_width), BF16), vmem((reps, cap, out_width), BF16),
        vmem(queries.shape, F32), vmem(queries.shape, F32), vmem((rows, HD), F32), vmem((rows, out_width), F32),
        vmem((rows, out_width), BF16), vmem(queries.shape, BF16), dma((1 + out_width // HD,)),
        dma((tps,)), dma((tps,)), dma((reps,)), dma((reps,)), dma((reps,)), dma((reps,)),
        dma((tps, reps)), dma((tps, reps)), dma((reps,)), dma((reps,)),
    ]
    anywhere = pl.BlockSpec(memory_space=pl.ANY)
    results = (jax.ShapeDtypeStruct((rows, out_width), BF16), jax.ShapeDtypeStruct(queries.shape, BF16))
    value, attended = pl.pallas_call(
        functools.partial(kernel, reps, tps, cap, stored, rank),
        out_shape=results,
        in_specs=[anywhere] * 11,
        out_specs=(anywhere, anywhere),
        scratch_shapes=scratch,
        compiler_params=pltpu.CompilerParams(
            collective_id=0, has_side_effects=True, vmem_limit_bytes=60 * 1024 * 1024
        ),
    )(
        hidden, fresh_token_keys, lengths.reshape(1, rows), row_adapter_index.reshape(1, rows),
        adapter_table_place.reshape(1, -1), queries, cached_key_rows, cached_value_rows, w,
        adapter_down_factor.reshape(stored * rank, width), adapter_up_factor.reshape(stored * rank, out_width),
    )
    return pl.pallas_call(
        hand_over,
        out_shape=results,
        in_specs=[anywhere] * 2,
        out_specs=(anywhere, anywhere),
        scratch_shapes=[dma((2,))],
        compiler_params=pltpu.CompilerParams(vmem_limit_bytes=60 * 1024 * 1024),
    )(value, attended)


def solution(mesh):
    return jax.shard_map(
        shards_fn,
        mesh=mesh,
        in_specs=(
            P(("groups", "rep"), "tp"),
            P(("groups", "rep"), "tp"),
            P(("groups", "rep"), "tp"),
            P(("groups", "rep"), None, "tp"),
            P(("groups", "rep"), None, "tp"),
            P(("groups", "rep")),
            P(("groups", "rep")),
            P("groups"),
            P(None, "tp"),
            P(("groups", "rep"), None, "tp"),
            P(("groups", "rep"), None, "tp"),
        ),
        out_specs=(P(("groups", "rep"), "tp"), P(("groups", "rep"), "tp")),
        check_vma=False,
    )
```

```python
import functools

import jax
import jax.numpy as jnp
from jax import lax
from jax.experimental import pallas as pl
from jax.experimental.pallas import tpu as pltpu
from jax.sharding import PartitionSpec as P

HD = 128
ROW_BLOCK = 16
ADAPTER_SCALE = 2.0
MASKED = -1e30
F32, BF16 = jnp.float32, jnp.bfloat16
NT = (((1,), (1,)), ((), ()))
TN = (((0,), (0,)), ((), ()))
NN = (((1,), (0,)), ((), ()))


def dot(a, b, dims=NN):
    return lax.dot_general(a, b, dims, preferred_element_type=F32)


def iota(shape, dim):
    return lax.broadcasted_iota(jnp.int32, shape, dim)


def kernel(
    reps, tps, cap, stored, rank,
    hidden_hbm, fresh_hbm, lengths_hbm, index_hbm, places_hbm, q_hbm, k_hbm, v_hbm, w_hbm, down_hbm, up_hbm,
    value_out, mixed_out, own_out,
    hidden, fresh, lengths, index, places,
    q_v, k_v, v_v, w_v, down_v, up_v, local_sem,
    shards, out_rows, in_rows, out_ids, in_ids, slots, part, parts, out_delta, in_delta,
    mixed_v, own_v, length_v, value_v, value_b, store_sem,
    gather_send, gather_recv, row_send, row_recv, id_send, id_recv,
    part_send, part_recv, delta_send, delta_recv,
):
    me_r, me_t = lax.axis_index("rep"), lax.axis_index("tp")
    rows, kv_local = hidden.shape[0], fresh.shape[1] // HD
    group = q_v.shape[1] // fresh.shape[1]
    positions = k_v.shape[1]
    span = ROW_BLOCK * positions

    def rep_at(k):
        return lax.rem(me_r + k, reps)

    rep_sibling = me_r + 1 - 2 * lax.rem(me_r, 2)

    def rep_near(i):
        odd = lax.rem(i, 2)
        return lax.rem(odd * rep_sibling + (1 - odd) * me_r + 2 * (i // 2), reps)

    def tp_at(k):
        return lax.rem(me_t + k, tps)

    sibling = me_t + 1 - 2 * lax.rem(me_t, 2)

    loads = [
        pltpu.make_async_copy(src, dst, local_sem.at[n])
        for n, (src, dst) in enumerate(
            (
                (q_hbm, q_v), (k_hbm, k_v), (v_hbm, v_v), (down_hbm, down_v), (w_hbm, w_v), (up_hbm, up_v),
                (index_hbm, index), (places_hbm, places), (hidden_hbm, hidden), (lengths_hbm, lengths), (fresh_hbm, fresh),
            )
        )
    ]
    for n in (6, 7, 8, 9, 10, 0, 1, 2, 3, 5, 4):
        loads[n].start()

    barrier = pltpu.get_barrier_semaphore()

    def greet_rep(k, c):
        pl.semaphore_signal(barrier, inc=1, device_id={"rep": rep_at(k)}, device_id_type=pl.DeviceIdType.MESH)
        return c

    def greet_tp(k, c):
        pl.semaphore_signal(barrier, inc=1, device_id={"tp": tp_at(k)}, device_id_type=pl.DeviceIdType.MESH)
        return c

    lax.fori_loop(1, reps, greet_rep, 0)
    lax.fori_loop(1, tps, greet_tp, 0)

    loads[6].wait()
    loads[7].wait()
    adapters = places.shape[1]
    place = places[...].astype(F32)
    owner_tab = jnp.floor((place + 0.5) / stored)
    inner_tab = place - owner_tab * stored
    hot = (iota((adapters, rows), 0) == index[...]).astype(F32).astype(BF16)
    owner = dot(jnp.broadcast_to(owner_tab, (8, adapters)).astype(BF16), hot)
    inner = dot(jnp.broadcast_to(inner_tab, (8, adapters)).astype(BF16), hot).astype(BF16)
    rep_pad = max(8, reps)
    owner_row = owner[0:1, :]
    owner_hot = (iota((rep_pad, rows), 0).astype(F32) == owner_row).astype(F32)
    earlier = (iota((rows, rows), 0) < iota((rows, rows), 1)).astype(F32).astype(BF16)
    before = dot(owner_hot.astype(BF16), earlier)
    position = jnp.sum(before * owner_hot, axis=0, keepdims=True)
    slot_iota = iota((rows, rows), 0).astype(F32)

    def gather_copy(src, to, q, n):
        return pltpu.make_async_remote_copy(
            src_ref=src, dst_ref=shards.at[q], send_sem=gather_send.at[n], recv_sem=gather_recv.at[q],
            device_id={"tp": to}, device_id_type=pl.DeviceIdType.MESH,
        )

    def row_copy(d):
        return pltpu.make_async_remote_copy(
            src_ref=out_rows.at[d], dst_ref=in_rows.at[me_r], send_sem=row_send.at[d], recv_sem=row_recv.at[me_r],
            device_id={"rep": d}, device_id_type=pl.DeviceIdType.MESH,
        )

    def id_copy(d):
        return pltpu.make_async_remote_copy(
            src_ref=out_ids.at[d], dst_ref=in_ids.at[me_r], send_sem=id_send.at[d], recv_sem=id_recv.at[me_r],
            device_id={"rep": d}, device_id_type=pl.DeviceIdType.MESH,
        )

    def row_arrival(s):
        return pltpu.make_async_remote_copy(
            src_ref=out_rows.at[s], dst_ref=in_rows.at[s], send_sem=row_send.at[s], recv_sem=row_recv.at[s],
            device_id={"rep": s}, device_id_type=pl.DeviceIdType.MESH,
        )

    def id_arrival(s):
        return pltpu.make_async_remote_copy(
            src_ref=out_ids.at[s], dst_ref=in_ids.at[s], send_sem=id_send.at[s], recv_sem=id_recv.at[s],
            device_id={"rep": s}, device_id_type=pl.DeviceIdType.MESH,
        )

    def fill(d):
        member = jnp.where(owner_row == d.astype(F32), position, -1.0)
        dispatch = (slot_iota == member).astype(F32).astype(BF16)
        slots[d] = dispatch
        return dispatch

    loads[8].wait()
    pl.semaphore_wait(barrier, reps - 1 + tps - 1)

    def send_rows(i, c):
        d = rep_near(1 + i)
        dispatch = fill(d)
        out_rows[d] = dot(dispatch[:cap], hidden[...]).astype(BF16)
        row_copy(d).start()
        out_ids[d] = dot(inner, dispatch, NT)
        id_copy(d).start()
        return c

    lax.fori_loop(0, reps - 1, send_rows, 0)

    half = tps // 2
    gather_copy(hidden, sibling, me_t, 0).start()
    for k in range(1, half):
        gather_copy(hidden, tp_at(2 * k), me_t, k).start()

    dispatch = fill(me_r)
    in_rows[me_r] = dot(dispatch[:cap], hidden[...]).astype(BF16)
    in_ids[me_r] = dot(inner, dispatch, NT)

    loads[9].wait()
    diagonal = iota((rows, rows), 0) == iota((rows, rows), 1)
    length_col = jnp.sum(jnp.where(diagonal, lengths[...].astype(F32), 0.0), axis=1, keepdims=True)
    length_v[...] = jnp.broadcast_to(length_col, (rows, HD))

    inverse = 1.0 / HD**0.5
    loads[0].wait()
    loads[1].wait()
    loads[2].wait()
    loads[10].wait()

    def attend(b, c):
        at = pl.ds(pl.multiple_of(b * ROW_BLOCK, ROW_BLOCK), ROW_BLOCK)
        column = iota((ROW_BLOCK, span), 1).astype(F32)
        low = (iota((ROW_BLOCK, span), 0) * positions).astype(F32)
        high = low + length_v[at, 0:1]
        bias = jnp.where((column >= low) & (column < high), 0.0, MASKED)
        lane = iota((ROW_BLOCK, HD), 1)
        own_lanes = jnp.zeros((ROW_BLOCK, HD), F32)
        for g in range(kv_local):
            feats = slice(g * HD, (g + 1) * HD)
            heads = [slice((g * group + j) * HD, (g * group + j + 1) * HD) for j in range(group)]
            query = jnp.concatenate([q_v[at, h] for h in heads], axis=0)
            keys = k_v[at, :, feats].reshape(span, HD)
            values = v_v[at, :, feats].reshape(span, HD)
            scores = dot(query, keys, NT).reshape(group, ROW_BLOCK, span) * inverse + bias[None]
            own = (
                jnp.sum(
                    query.astype(F32).reshape(group, ROW_BLOCK, HD) * fresh[at, feats].astype(F32)[None],
                    axis=-1, keepdims=True,
                )
                * inverse
            )
            top = jnp.maximum(jnp.max(scores, axis=-1, keepdims=True), own)
            expo = jnp.exp(scores - top)
            own_expo = jnp.exp(own - top)
            scale = 1.0 / (jnp.sum(expo, axis=-1, keepdims=True) + own_expo)
            weights = (expo * scale).astype(BF16).reshape(group * ROW_BLOCK, span)
            own_weight = (own_expo * scale).astype(BF16).astype(F32)
            mixed = dot(weights, values)
            for j, h in enumerate(heads):
                mixed_v[at, h] = mixed[j * ROW_BLOCK:(j + 1) * ROW_BLOCK]
                own_lanes = jnp.where(lane == g * group + j, own_weight[j], own_lanes)
        own_v[at, :] = own_lanes
        return c


    def part_copy(k, s):
        return pltpu.make_async_remote_copy(
            src_ref=part.at[s], dst_ref=parts.at[me_t, s], send_sem=part_send.at[k, s],
            recv_sem=part_recv.at[me_t, s], device_id={"tp": tp_at(k)}, device_id_type=pl.DeviceIdType.MESH,
        )

    def part_arrival(k, s):
        q = tp_at(k)
        return pltpu.make_async_remote_copy(
            src_ref=part.at[s], dst_ref=parts.at[q, s], send_sem=part_send.at[k, s],
            recv_sem=part_recv.at[q, s], device_id={"tp": q}, device_id_type=pl.DeviceIdType.MESH,
        )

    def delta_copy(s):
        return pltpu.make_async_remote_copy(
            src_ref=out_delta.at[s], dst_ref=in_delta.at[me_r], send_sem=delta_send.at[s],
            recv_sem=delta_recv.at[me_r], device_id={"rep": s}, device_id_type=pl.DeviceIdType.MESH,
        )

    def delta_arrival(s):
        return pltpu.make_async_remote_copy(
            src_ref=out_delta.at[s], dst_ref=in_delta.at[s], send_sem=delta_send.at[s],
            recv_sem=delta_recv.at[s], device_id={"rep": s}, device_id_type=pl.DeviceIdType.MESH,
        )

    def chosen(s):
        return iota((stored, rank, cap), 0).astype(F32) == in_ids[s][0:1, :cap].reshape(1, 1, cap)

    def shrink(s):
        full = dot(down_v[...], in_rows[s], NT).reshape(stored, rank, cap)
        part[s] = jnp.sum(jnp.where(chosen(s), full, 0.0), axis=0)
        for k in range(1, tps):
            part_copy(k, s).start()

    def expand(s):
        total = part[s]
        for k in range(1, tps):
            part_arrival(k, s).wait_recv()
            total = total + parts[tp_at(k), s]
        total = total.astype(BF16).astype(F32)
        spread = jnp.where(chosen(s), total[None], 0.0).reshape(stored * rank, cap).astype(BF16)
        return (ADAPTER_SCALE * dot(spread, up_v[...], TN)).astype(BF16)

    def forward():
        for k in range(1, half):
            q = tp_at(2 * k)
            gather_copy(hidden, q, q, 0).wait_recv()
            gather_copy(shards.at[q], sibling, q, half + k).start()
        loads[4].wait()
        value_v[...] = dot(hidden[...], w_v[me_t])
        in_delta[me_r] = expand(me_r)

    def finish_base():
        base = value_v[...]
        for k in range(1, half):
            q = tp_at(2 * k)
            base = base + dot(shards[q], w_v[q])
        for k in range(half):
            q = lax.rem(sibling + 2 * k, tps)
            gather_copy(hidden, q, q, 0).wait_recv()
            base = base + dot(shards[q], w_v[q])
        value_v[...] = base + dot(slots[me_r][:cap], in_delta[me_r], TN)

    def step(i, c):
        s = rep_near(i)
        row_arrival(s).wait_recv()
        id_arrival(s).wait_recv()
        shrink(s)
        pl.when(i == 1)(forward)
        pl.when(i == min(2, reps - 1))(finish_base)
        out_delta[s] = expand(s)
        delta_copy(s).start()
        return c

    blocks = rows // ROW_BLOCK
    early = blocks // 2
    lax.fori_loop(0, early, attend, 0)
    loads[3].wait()
    loads[5].wait()
    shrink(me_r)
    lax.fori_loop(early, blocks, attend, 0)
    store_mixed = pltpu.make_async_copy(mixed_v, mixed_out, store_sem.at[1])
    store_own = pltpu.make_async_copy(own_v, own_out, store_sem.at[2])
    store_mixed.start()
    store_own.start()
    lax.fori_loop(1, reps, step, 0)

    def collect(i, c):
        s = rep_near(i)
        delta_arrival(s).wait_recv()
        value_v[...] += dot(slots[s][:cap], in_delta[s], TN)
        return c

    lax.fori_loop(1, reps, collect, 0)

    value = value_v[...].astype(BF16)
    value_b[...] = value
    store_value = pltpu.make_async_copy(value_b, value_out, store_sem.at[0])
    store_value.start()

    gather_copy(hidden, sibling, me_t, 0).wait_send()
    for k in range(1, half):
        gather_copy(hidden, sibling, me_t, k).wait_send()
        gather_copy(hidden, sibling, me_t, half + k).wait_send()

    def drain(i, c):
        d = rep_at(i)
        row_copy(d).wait_send()
        id_copy(d).wait_send()
        delta_copy(d).wait_send()
        return c

    lax.fori_loop(1, reps, drain, 0)

    def drain_parts(s, c):
        for k in range(1, tps):
            part_copy(k, s).wait_send()
        return c

    lax.fori_loop(0, reps, drain_parts, 0)
    for store in (store_value, store_mixed, store_own):
        store.wait()


def combine(value_hbm, mixed_hbm, own_hbm, value_out, attended_out, value_v, mixed_v, own_v, attended_v, sem):
    kv_local = value_v.shape[1] // HD
    width = mixed_v.shape[1] // kv_local
    parts = [slice(g * width, (g + 1) * width) for g in range(kv_local)]
    loads = [pltpu.make_async_copy(value_hbm, value_v, sem.at[0]), pltpu.make_async_copy(own_hbm, own_v, sem.at[1])]
    loads += [pltpu.make_async_copy(mixed_hbm.at[:, p], mixed_v.at[:, p], sem.at[2 + g]) for g, p in enumerate(parts)]
    for load in loads:
        load.start()
    loads[0].wait()
    stores = [pltpu.make_async_copy(value_v, value_out, sem.at[2 + kv_local])]
    stores[0].start()
    loads[1].wait()
    for g, p in enumerate(parts):
        loads[2 + g].wait()
        value = value_v[:, g * HD:(g + 1) * HD].astype(F32)
        for j in range(width // HD):
            n = g * (width // HD) + j
            h = slice(n * HD, (n + 1) * HD)
            attended_v[:, h] = (mixed_v[:, h] + own_v[:, n:n + 1] * value).astype(BF16)
        stores.append(pltpu.make_async_copy(attended_v.at[:, p], attended_out.at[:, p], sem.at[3 + kv_local + g]))
        stores[-1].start()
    for store in stores:
        store.wait()


def shards_fn(
    hidden, queries, fresh_token_keys, cached_key_rows, cached_value_rows, lengths, row_adapter_index,
    adapter_table_place, value_projection_matrix, adapter_down_factor, adapter_up_factor,
):
    reps, tps = lax.axis_size("rep"), lax.axis_size("tp")
    rows, width = hidden.shape
    stored, rank, _ = adapter_down_factor.shape
    out_width = adapter_up_factor.shape[2]
    cap = max(2, (2 * rows + reps - 1) // reps)
    dma = pltpu.SemaphoreType.DMA
    vmem = pltpu.VMEM
    w = value_projection_matrix.reshape(tps, width, out_width)
    adapters = adapter_table_place.shape[0]
    scratch = [
        vmem(hidden.shape, BF16), vmem(fresh_token_keys.shape, BF16),
        vmem((1, rows), jnp.int32), vmem((1, rows), jnp.int32), vmem((1, adapters), jnp.int32),
        vmem(queries.shape, BF16), vmem(cached_key_rows.shape, BF16), vmem(cached_value_rows.shape, BF16),
        vmem(w.shape, BF16), vmem((stored * rank, width), BF16), vmem((stored * rank, out_width), BF16), dma((11,)),
        vmem((tps, rows, width), BF16),
        vmem((reps, cap, width), BF16), vmem((reps, cap, width), BF16),
        vmem((reps, 8, rows), F32), vmem((reps, 8, rows), F32),
        vmem((reps, rows, rows), BF16),
        vmem((reps, rank, cap), F32), vmem((tps, reps, rank, cap), F32),
        vmem((reps, cap, out_width), BF16), vmem((reps, cap, out_width), BF16),
        vmem(queries.shape, F32), vmem((rows, HD), F32), vmem((rows, HD), F32), vmem((rows, out_width), F32),
        vmem((rows, out_width), BF16), dma((3,)),
        dma((tps,)), dma((tps,)), dma((reps,)), dma((reps,)), dma((reps,)), dma((reps,)),
        dma((tps, reps)), dma((tps, reps)), dma((reps,)), dma((reps,)),
    ]
    anywhere = pl.BlockSpec(memory_space=pl.ANY)
    results = (jax.ShapeDtypeStruct((rows, out_width), BF16), jax.ShapeDtypeStruct(queries.shape, BF16))
    value, mixed, own = pl.pallas_call(
        functools.partial(kernel, reps, tps, cap, stored, rank),
        out_shape=(
            results[0], jax.ShapeDtypeStruct(queries.shape, F32), jax.ShapeDtypeStruct((rows, HD), F32),
        ),
        in_specs=[anywhere] * 11,
        out_specs=(anywhere,) * 3,
        scratch_shapes=scratch,
        compiler_params=pltpu.CompilerParams(
            collective_id=0, has_side_effects=True, vmem_limit_bytes=60 * 1024 * 1024
        ),
    )(
        hidden, fresh_token_keys, lengths.reshape(1, rows), row_adapter_index.reshape(1, rows),
        adapter_table_place.reshape(1, -1), queries, cached_key_rows, cached_value_rows, w,
        adapter_down_factor.reshape(stored * rank, width), adapter_up_factor.reshape(stored * rank, out_width),
    )
    return pl.pallas_call(
        combine,
        out_shape=results,
        in_specs=[anywhere] * 3,
        out_specs=(anywhere, anywhere),
        scratch_shapes=[
            vmem((rows, out_width), BF16), vmem(queries.shape, F32), vmem((rows, HD), F32), vmem(queries.shape, BF16),
            dma((3 + 2 * (out_width // HD),)),
        ],
        compiler_params=pltpu.CompilerParams(vmem_limit_bytes=60 * 1024 * 1024),
    )(value, mixed, own)


def solution(mesh):
    return jax.shard_map(
        shards_fn,
        mesh=mesh,
        in_specs=(
            P(("groups", "rep"), "tp"),
            P(("groups", "rep"), "tp"),
            P(("groups", "rep"), "tp"),
            P(("groups", "rep"), None, "tp"),
            P(("groups", "rep"), None, "tp"),
            P(("groups", "rep")),
            P(("groups", "rep")),
            P("groups"),
            P(None, "tp"),
            P(("groups", "rep"), None, "tp"),
            P(("groups", "rep"), None, "tp"),
        ),
        out_specs=(P(("groups", "rep"), "tp"), P(("groups", "rep"), "tp")),
        check_vma=False,
    )
```

```python
import functools

import jax
import jax.numpy as jnp
from jax import lax
from jax.experimental import pallas as pl
from jax.experimental.pallas import tpu as pltpu
from jax.sharding import PartitionSpec as P

HD = 128
ROW_BLOCK = 16
ADAPTER_SCALE = 2.0
MASKED = -1e30
F32, BF16 = jnp.float32, jnp.bfloat16
NT = (((1,), (1,)), ((), ()))
TN = (((0,), (0,)), ((), ()))
NN = (((1,), (0,)), ((), ()))


def dot(a, b, dims=NN):
    return lax.dot_general(a, b, dims, preferred_element_type=F32)


def iota(shape, dim):
    return lax.broadcasted_iota(jnp.int32, shape, dim)


def kernel(
    reps, tps, cap, stored, rank,
    hidden_hbm, fresh_hbm, lengths_hbm, index_hbm, places_hbm, q_hbm, k_hbm, v_hbm, w_hbm, down_hbm, up_hbm,
    value_b, mixed_v, own_v,
    hidden, fresh, lengths, index, places,
    q_v, k_v, v_v, w_v, down_v, up_v, local_sem,
    shards, out_rows, in_rows, out_ids, in_ids, slots, part, parts, out_delta, in_delta,
    length_v, value_v,
    gather_send, gather_recv, row_send, row_recv, id_send, id_recv,
    part_send, part_recv, delta_send, delta_recv,
):
    me_r, me_t = lax.axis_index("rep"), lax.axis_index("tp")
    rows, kv_local = hidden.shape[0], fresh.shape[1] // HD
    group = q_v.shape[1] // fresh.shape[1]
    positions = k_v.shape[1]
    span = ROW_BLOCK * positions

    def rep_at(k):
        return lax.rem(me_r + k, reps)

    rep_sibling = me_r + 1 - 2 * lax.rem(me_r, 2)

    def rep_near(i):
        odd = lax.rem(i, 2)
        return lax.rem(odd * rep_sibling + (1 - odd) * me_r + 2 * (i // 2), reps)

    def tp_at(k):
        return lax.rem(me_t + k, tps)

    sibling = me_t + 1 - 2 * lax.rem(me_t, 2)

    loads = [
        pltpu.make_async_copy(src, dst, local_sem.at[n])
        for n, (src, dst) in enumerate(
            (
                (q_hbm, q_v), (k_hbm, k_v), (v_hbm, v_v), (down_hbm, down_v), (w_hbm, w_v), (up_hbm, up_v),
                (index_hbm, index), (places_hbm, places), (hidden_hbm, hidden), (lengths_hbm, lengths), (fresh_hbm, fresh),
            )
        )
    ]
    for n in (6, 7, 8):
        loads[n].start()

    barrier = pltpu.get_barrier_semaphore()

    def greet_rep(k, c):
        pl.semaphore_signal(barrier, inc=1, device_id={"rep": rep_at(k)}, device_id_type=pl.DeviceIdType.MESH)
        return c

    def greet_tp(k, c):
        pl.semaphore_signal(barrier, inc=1, device_id={"tp": tp_at(k)}, device_id_type=pl.DeviceIdType.MESH)
        return c

    lax.fori_loop(1, reps, greet_rep, 0)
    lax.fori_loop(1, tps, greet_tp, 0)

    loads[6].wait()
    loads[7].wait()
    adapters = places.shape[1]
    place = places[...].astype(F32)
    owner_tab = jnp.floor((place + 0.5) / stored)
    inner_tab = place - owner_tab * stored
    hot = (iota((adapters, rows), 0) == index[...]).astype(F32).astype(BF16)
    owner = dot(jnp.broadcast_to(owner_tab, (8, adapters)).astype(BF16), hot)
    inner = dot(jnp.broadcast_to(inner_tab, (8, adapters)).astype(BF16), hot).astype(BF16)
    rep_pad = max(8, reps)
    owner_row = owner[0:1, :]
    owner_hot = (iota((rep_pad, rows), 0).astype(F32) == owner_row).astype(F32)
    earlier = (iota((rows, rows), 0) < iota((rows, rows), 1)).astype(F32).astype(BF16)
    before = dot(owner_hot.astype(BF16), earlier)
    position = jnp.sum(before * owner_hot, axis=0, keepdims=True)
    slot_iota = iota((rows, rows), 0).astype(F32)

    def gather_copy(src, to, q, n):
        return pltpu.make_async_remote_copy(
            src_ref=src, dst_ref=shards.at[q], send_sem=gather_send.at[n], recv_sem=gather_recv.at[q],
            device_id={"tp": to}, device_id_type=pl.DeviceIdType.MESH,
        )

    def row_copy(d):
        return pltpu.make_async_remote_copy(
            src_ref=out_rows.at[d], dst_ref=in_rows.at[me_r], send_sem=row_send.at[d], recv_sem=row_recv.at[me_r],
            device_id={"rep": d}, device_id_type=pl.DeviceIdType.MESH,
        )

    def id_copy(d):
        return pltpu.make_async_remote_copy(
            src_ref=out_ids.at[d], dst_ref=in_ids.at[me_r], send_sem=id_send.at[d], recv_sem=id_recv.at[me_r],
            device_id={"rep": d}, device_id_type=pl.DeviceIdType.MESH,
        )

    def row_arrival(s):
        return pltpu.make_async_remote_copy(
            src_ref=out_rows.at[s], dst_ref=in_rows.at[s], send_sem=row_send.at[s], recv_sem=row_recv.at[s],
            device_id={"rep": s}, device_id_type=pl.DeviceIdType.MESH,
        )

    def id_arrival(s):
        return pltpu.make_async_remote_copy(
            src_ref=out_ids.at[s], dst_ref=in_ids.at[s], send_sem=id_send.at[s], recv_sem=id_recv.at[s],
            device_id={"rep": s}, device_id_type=pl.DeviceIdType.MESH,
        )

    def fill(d):
        member = jnp.where(owner_row == d.astype(F32), position, -1.0)
        dispatch = (slot_iota == member).astype(F32).astype(BF16)
        slots[d] = dispatch
        return dispatch

    loads[8].wait()
    for n in (9, 10, 0, 1, 2, 3, 5, 4):
        loads[n].start()
    pl.semaphore_wait(barrier, reps - 1 + tps - 1)

    direct = reps // 2

    def send_rows(i, c):
        d = rep_near(1 + i)
        dispatch = fill(d)
        out_rows[d] = dot(dispatch[:cap], hidden[...]).astype(BF16)
        pl.when(i < direct)(row_copy(d).start)
        out_ids[d] = dot(inner, dispatch, NT)
        id_copy(d).start()
        return c

    lax.fori_loop(0, reps - 1, send_rows, 0)

    half = tps // 2
    gather_copy(hidden, sibling, me_t, 0).start()
    for k in range(1, half):
        gather_copy(hidden, tp_at(2 * k), me_t, k).start()

    dispatch = fill(me_r)
    in_rows[me_r] = dot(dispatch[:cap], hidden[...]).astype(BF16)
    in_ids[me_r] = dot(inner, dispatch, NT)

    loads[9].wait()
    diagonal = iota((rows, rows), 0) == iota((rows, rows), 1)
    length_col = jnp.sum(jnp.where(diagonal, lengths[...].astype(F32), 0.0), axis=1, keepdims=True)
    length_v[...] = jnp.broadcast_to(length_col, (rows, HD))

    inverse = 1.0 / HD**0.5
    loads[0].wait()
    loads[1].wait()
    loads[2].wait()
    loads[10].wait()

    def attend(b, c):
        at = pl.ds(pl.multiple_of(b * ROW_BLOCK, ROW_BLOCK), ROW_BLOCK)
        column = iota((ROW_BLOCK, span), 1).astype(F32)
        low = (iota((ROW_BLOCK, span), 0) * positions).astype(F32)
        high = low + length_v[at, 0:1]
        bias = jnp.where((column >= low) & (column < high), 0.0, MASKED)
        lane = iota((ROW_BLOCK, HD), 1)
        own_lanes = jnp.zeros((ROW_BLOCK, HD), F32)
        for g in range(kv_local):
            feats = slice(g * HD, (g + 1) * HD)
            heads = [slice((g * group + j) * HD, (g * group + j + 1) * HD) for j in range(group)]
            query = jnp.concatenate([q_v[at, h] for h in heads], axis=0)
            keys = k_v[at, :, feats].reshape(span, HD)
            values = v_v[at, :, feats].reshape(span, HD)
            scores = dot(query, keys, NT).reshape(group, ROW_BLOCK, span) * inverse + bias[None]
            own = (
                jnp.sum(
                    query.astype(F32).reshape(group, ROW_BLOCK, HD) * fresh[at, feats].astype(F32)[None],
                    axis=-1, keepdims=True,
                )
                * inverse
            )
            top = jnp.maximum(jnp.max(scores, axis=-1, keepdims=True), own)
            expo = jnp.exp(scores - top)
            own_expo = jnp.exp(own - top)
            scale = 1.0 / (jnp.sum(expo, axis=-1, keepdims=True) + own_expo)
            weights = (expo * scale).astype(BF16).reshape(group * ROW_BLOCK, span)
            own_weight = (own_expo * scale).astype(BF16).astype(F32)
            mixed = dot(weights, values)
            for j, h in enumerate(heads):
                mixed_v[at, h] = mixed[j * ROW_BLOCK:(j + 1) * ROW_BLOCK]
                own_lanes = jnp.where(lane == g * group + j, own_weight[j], own_lanes)
        own_v[at, :] = own_lanes
        return c


    def part_copy(k, s):
        return pltpu.make_async_remote_copy(
            src_ref=part.at[s], dst_ref=parts.at[me_t, s], send_sem=part_send.at[k, s],
            recv_sem=part_recv.at[me_t, s], device_id={"tp": tp_at(k)}, device_id_type=pl.DeviceIdType.MESH,
        )

    def part_arrival(k, s):
        q = tp_at(k)
        return pltpu.make_async_remote_copy(
            src_ref=part.at[s], dst_ref=parts.at[q, s], send_sem=part_send.at[k, s],
            recv_sem=part_recv.at[q, s], device_id={"tp": q}, device_id_type=pl.DeviceIdType.MESH,
        )

    def delta_copy(s):
        return pltpu.make_async_remote_copy(
            src_ref=out_delta.at[s], dst_ref=in_delta.at[me_r], send_sem=delta_send.at[s],
            recv_sem=delta_recv.at[me_r], device_id={"rep": s}, device_id_type=pl.DeviceIdType.MESH,
        )

    def delta_arrival(s):
        return pltpu.make_async_remote_copy(
            src_ref=out_delta.at[s], dst_ref=in_delta.at[s], send_sem=delta_send.at[s],
            recv_sem=delta_recv.at[s], device_id={"rep": s}, device_id_type=pl.DeviceIdType.MESH,
        )

    def chosen(s):
        return iota((stored, rank, cap), 0).astype(F32) == in_ids[s][0:1, :cap].reshape(1, 1, cap)

    def shrink(s):
        full = dot(down_v[...], in_rows[s], NT).reshape(stored, rank, cap)
        part[s] = jnp.sum(jnp.where(chosen(s), full, 0.0), axis=0)
        for k in range(1, tps):
            part_copy(k, s).start()

    def expand(s):
        total = part[s]
        for k in range(1, tps):
            part_arrival(k, s).wait_recv()
            total = total + parts[tp_at(k), s]
        total = total.astype(BF16).astype(F32)
        spread = jnp.where(chosen(s), total[None], 0.0).reshape(stored * rank, cap).astype(BF16)
        return (ADAPTER_SCALE * dot(spread, up_v[...], TN)).astype(BF16)

    def forward():
        for k in range(1, half):
            q = tp_at(2 * k)
            gather_copy(hidden, q, q, 0).wait_recv()
            gather_copy(shards.at[q], sibling, q, half + k).start()
        loads[4].wait()
        value_v[...] = dot(hidden[...], w_v[me_t])
        in_delta[me_r] = expand(me_r)

    def finish_base():
        base = value_v[...]
        for k in range(1, half):
            q = tp_at(2 * k)
            base = base + dot(shards[q], w_v[q])
        for k in range(half):
            q = lax.rem(sibling + 2 * k, tps)
            gather_copy(hidden, q, q, 0).wait_recv()
            base = base + dot(shards[q], w_v[q])
        value_v[...] = base + dot(slots[me_r][:cap], in_delta[me_r], TN)

    def step(i, c):
        s = rep_near(i)
        row_arrival(s).wait_recv()
        id_arrival(s).wait_recv()
        shrink(s)
        pl.when(i == 1)(forward)
        pl.when(i == min(2, reps - 1))(finish_base)
        out_delta[s] = expand(s)
        delta_copy(s).start()
        return c

    blocks = rows // ROW_BLOCK
    early = blocks // 2
    lax.fori_loop(0, early, attend, 0)
    loads[3].wait()
    loads[5].wait()
    shrink(me_r)
    lax.fori_loop(early, blocks, attend, 0)

    def send_later(i, c):
        row_copy(rep_near(1 + i - 1)).wait_send()
        row_copy(rep_near(1 + i)).start()
        return c

    lax.fori_loop(direct, reps - 1, send_later, 0)
    lax.fori_loop(1, reps, step, 0)

    def collect(i, c):
        s = rep_near(i)
        delta_arrival(s).wait_recv()
        value_v[...] += dot(slots[s][:cap], in_delta[s], TN)
        return c

    lax.fori_loop(1, reps, collect, 0)

    value_b[...] = value_v[...].astype(BF16)

    gather_copy(hidden, sibling, me_t, 0).wait_send()
    for k in range(1, half):
        gather_copy(hidden, sibling, me_t, k).wait_send()
        gather_copy(hidden, sibling, me_t, half + k).wait_send()

    def drain(i, c):
        d = rep_near(i)
        pl.when((i < direct) | (i == reps - 1))(row_copy(d).wait_send)
        id_copy(d).wait_send()
        delta_copy(d).wait_send()
        return c

    lax.fori_loop(1, reps, drain, 0)

    def drain_parts(s, c):
        for k in range(1, tps):
            part_copy(k, s).wait_send()
        return c

    lax.fori_loop(0, reps, drain_parts, 0)


def combine(value_v, mixed_v, own_v, value_out, attended_out, attended_v, sem):
    kv_local = value_v.shape[1] // HD
    width = mixed_v.shape[1] // kv_local
    stores = [pltpu.make_async_copy(value_v, value_out, sem.at[0])]
    stores[0].start()
    for g in range(kv_local):
        value = value_v[:, g * HD:(g + 1) * HD].astype(F32)
        for j in range(width // HD):
            n = g * (width // HD) + j
            h = slice(n * HD, (n + 1) * HD)
            attended_v[:, h] = (mixed_v[:, h] + own_v[:, n:n + 1] * value).astype(BF16)
        p = slice(g * width, (g + 1) * width)
        stores.append(pltpu.make_async_copy(attended_v.at[:, p], attended_out.at[:, p], sem.at[1 + g]))
        stores[-1].start()
    for store in stores:
        store.wait()


def shards_fn(
    hidden, queries, fresh_token_keys, cached_key_rows, cached_value_rows, lengths, row_adapter_index,
    adapter_table_place, value_projection_matrix, adapter_down_factor, adapter_up_factor,
):
    reps, tps = lax.axis_size("rep"), lax.axis_size("tp")
    rows, width = hidden.shape
    stored, rank, _ = adapter_down_factor.shape
    out_width = adapter_up_factor.shape[2]
    cap = max(2, (2 * rows + reps - 1) // reps)
    dma = pltpu.SemaphoreType.DMA
    vmem = pltpu.VMEM
    w = value_projection_matrix.reshape(tps, width, out_width)
    adapters = adapter_table_place.shape[0]
    scratch = [
        vmem(hidden.shape, BF16), vmem(fresh_token_keys.shape, BF16),
        vmem((1, rows), jnp.int32), vmem((1, rows), jnp.int32), vmem((1, adapters), jnp.int32),
        vmem(queries.shape, BF16), vmem(cached_key_rows.shape, BF16), vmem(cached_value_rows.shape, BF16),
        vmem(w.shape, BF16), vmem((stored * rank, width), BF16), vmem((stored * rank, out_width), BF16), dma((11,)),
        vmem((tps, rows, width), BF16),
        vmem((reps, cap, width), BF16), vmem((reps, cap, width), BF16),
        vmem((reps, 8, rows), F32), vmem((reps, 8, rows), F32),
        vmem((reps, rows, rows), BF16),
        vmem((reps, rank, cap), F32), vmem((tps, reps, rank, cap), F32),
        vmem((reps, cap, out_width), BF16), vmem((reps, cap, out_width), BF16),
        vmem((rows, HD), F32), vmem((rows, out_width), F32),
        dma((tps,)), dma((tps,)), dma((reps,)), dma((reps,)), dma((reps,)), dma((reps,)),
        dma((tps, reps)), dma((tps, reps)), dma((reps,)), dma((reps,)),
    ]
    anywhere, inside = pl.BlockSpec(memory_space=pl.ANY), pl.BlockSpec(memory_space=pltpu.VMEM)
    results = (jax.ShapeDtypeStruct((rows, out_width), BF16), jax.ShapeDtypeStruct(queries.shape, BF16))
    value, mixed, own = pl.pallas_call(
        functools.partial(kernel, reps, tps, cap, stored, rank),
        out_shape=(
            vmem((rows, out_width), BF16), vmem(queries.shape, F32), vmem((rows, HD), F32),
        ),
        in_specs=[anywhere] * 11,
        out_specs=(inside,) * 3,
        scratch_shapes=scratch,
        compiler_params=pltpu.CompilerParams(
            collective_id=0, has_side_effects=True, vmem_limit_bytes=60 * 1024 * 1024
        ),
    )(
        hidden, fresh_token_keys, lengths.reshape(1, rows), row_adapter_index.reshape(1, rows),
        adapter_table_place.reshape(1, -1), queries, cached_key_rows, cached_value_rows, w,
        adapter_down_factor.reshape(stored * rank, width), adapter_up_factor.reshape(stored * rank, out_width),
    )
    return pl.pallas_call(
        combine,
        out_shape=results,
        in_specs=[inside] * 3,
        out_specs=(anywhere, anywhere),
        scratch_shapes=[vmem(queries.shape, BF16), dma((1 + out_width // HD,))],
        compiler_params=pltpu.CompilerParams(vmem_limit_bytes=16 * 1024 * 1024),
    )(value, mixed, own)


def solution(mesh):
    return jax.shard_map(
        shards_fn,
        mesh=mesh,
        in_specs=(
            P(("groups", "rep"), "tp"),
            P(("groups", "rep"), "tp"),
            P(("groups", "rep"), "tp"),
            P(("groups", "rep"), None, "tp"),
            P(("groups", "rep"), None, "tp"),
            P(("groups", "rep")),
            P(("groups", "rep")),
            P("groups"),
            P(None, "tp"),
            P(("groups", "rep"), None, "tp"),
            P(("groups", "rep"), None, "tp"),
        ),
        out_specs=(P(("groups", "rep"), "tp"), P(("groups", "rep"), "tp")),
        check_vma=False,
    )
```

```python
import functools

import jax
import jax.numpy as jnp
from jax import lax
from jax.experimental import pallas as pl
from jax.experimental.pallas import tpu as pltpu
from jax.sharding import PartitionSpec as P

HD = 128
ROW_BLOCK = 16
ADAPTER_SCALE = 2.0
MASKED = -1e30
F32, BF16 = jnp.float32, jnp.bfloat16
NT = (((1,), (1,)), ((), ()))
TN = (((0,), (0,)), ((), ()))
NN = (((1,), (0,)), ((), ()))


def dot(a, b, dims=NN):
    return lax.dot_general(a, b, dims, preferred_element_type=F32)


def iota(shape, dim):
    return lax.broadcasted_iota(jnp.int32, shape, dim)


def kernel(
    reps, tps, cap, stored, rank,
    hidden_hbm, fresh_hbm, lengths_hbm, index_hbm, places_hbm, q_hbm, k_hbm, v_hbm, w_hbm, down_hbm, up_hbm,
    value_b, mixed_v, own_v,
    hidden, fresh, lengths, index, places,
    q_v, k_v, v_v, w_v, down_v, up_v, local_sem,
    shards, out_rows, in_rows, out_ids, in_ids, slots, part, parts, out_delta, in_delta,
    length_v, value_v,
    gather_send, gather_recv, row_send, row_recv, id_send, id_recv,
    part_send, part_recv, delta_send, delta_recv,
):
    me_r, me_t = lax.axis_index("rep"), lax.axis_index("tp")
    rows, kv_local = hidden.shape[0], fresh.shape[1] // HD
    group = q_v.shape[1] // fresh.shape[1]
    positions = k_v.shape[1]
    span = ROW_BLOCK * positions

    def rep_at(k):
        return lax.rem(me_r + k, reps)

    rep_sibling = me_r + 1 - 2 * lax.rem(me_r, 2)

    def rep_near(i):
        odd = lax.rem(i, 2)
        return lax.rem(odd * rep_sibling + (1 - odd) * me_r + 2 * (i // 2), reps)

    def tp_at(k):
        return lax.rem(me_t + k, tps)

    sibling = me_t + 1 - 2 * lax.rem(me_t, 2)

    loads = [
        pltpu.make_async_copy(src, dst, local_sem.at[n])
        for n, (src, dst) in enumerate(
            (
                (q_hbm, q_v), (k_hbm, k_v), (v_hbm, v_v), (down_hbm, down_v), (w_hbm, w_v), (up_hbm, up_v),
                (index_hbm, index), (places_hbm, places), (hidden_hbm, hidden), (lengths_hbm, lengths), (fresh_hbm, fresh),
            )
        )
    ]
    for n in (6, 7, 8):
        loads[n].start()

    barrier = pltpu.get_barrier_semaphore()

    def greet_rep(k, c):
        pl.semaphore_signal(barrier, inc=1, device_id={"rep": rep_at(k)}, device_id_type=pl.DeviceIdType.MESH)
        return c

    def greet_tp(k, c):
        pl.semaphore_signal(barrier, inc=1, device_id={"tp": tp_at(k)}, device_id_type=pl.DeviceIdType.MESH)
        return c

    lax.fori_loop(1, reps, greet_rep, 0)
    lax.fori_loop(1, tps, greet_tp, 0)

    loads[6].wait()
    loads[7].wait()
    adapters = places.shape[1]
    place = places[...].astype(F32)
    owner_tab = jnp.floor((place + 0.5) / stored)
    inner_tab = place - owner_tab * stored
    hot = (iota((adapters, rows), 0) == index[...]).astype(F32).astype(BF16)
    owner = dot(jnp.broadcast_to(owner_tab, (8, adapters)).astype(BF16), hot)
    inner = dot(jnp.broadcast_to(inner_tab, (8, adapters)).astype(BF16), hot).astype(BF16)
    rep_pad = max(8, reps)
    owner_row = owner[0:1, :]
    owner_hot = (iota((rep_pad, rows), 0).astype(F32) == owner_row).astype(F32)
    earlier = (iota((rows, rows), 0) < iota((rows, rows), 1)).astype(F32).astype(BF16)
    before = dot(owner_hot.astype(BF16), earlier)
    position = jnp.sum(before * owner_hot, axis=0, keepdims=True)
    slot_iota = iota((rows, rows), 0).astype(F32)

    def gather_copy(src, to, q, n):
        return pltpu.make_async_remote_copy(
            src_ref=src, dst_ref=shards.at[q], send_sem=gather_send.at[n], recv_sem=gather_recv.at[q],
            device_id={"tp": to}, device_id_type=pl.DeviceIdType.MESH,
        )

    def row_copy(d):
        return pltpu.make_async_remote_copy(
            src_ref=out_rows.at[d], dst_ref=in_rows.at[me_r], send_sem=row_send.at[d], recv_sem=row_recv.at[me_r],
            device_id={"rep": d}, device_id_type=pl.DeviceIdType.MESH,
        )

    def id_copy(d):
        return pltpu.make_async_remote_copy(
            src_ref=out_ids.at[d], dst_ref=in_ids.at[me_r], send_sem=id_send.at[d], recv_sem=id_recv.at[me_r],
            device_id={"rep": d}, device_id_type=pl.DeviceIdType.MESH,
        )

    def row_arrival(s):
        return pltpu.make_async_remote_copy(
            src_ref=out_rows.at[s], dst_ref=in_rows.at[s], send_sem=row_send.at[s], recv_sem=row_recv.at[s],
            device_id={"rep": s}, device_id_type=pl.DeviceIdType.MESH,
        )

    def id_arrival(s):
        return pltpu.make_async_remote_copy(
            src_ref=out_ids.at[s], dst_ref=in_ids.at[s], send_sem=id_send.at[s], recv_sem=id_recv.at[s],
            device_id={"rep": s}, device_id_type=pl.DeviceIdType.MESH,
        )

    def fill(d):
        member = jnp.where(owner_row == d.astype(F32), position, -1.0)
        dispatch = (slot_iota == member).astype(F32).astype(BF16)
        slots[d] = dispatch
        return dispatch

    loads[8].wait()
    for n in (9, 10, 0, 1, 2, 3, 5, 4):
        loads[n].start()
    pl.semaphore_wait(barrier, reps - 1 + tps - 1)

    direct = reps // 2

    def send_rows(i, c):
        d = rep_near(jnp.where(i < direct, direct - i, 1 + i))
        dispatch = fill(d)
        out_rows[d] = dot(dispatch[:cap], hidden[...]).astype(BF16)
        pl.when(i < direct)(row_copy(d).start)
        out_ids[d] = dot(inner, dispatch, NT)
        id_copy(d).start()
        return c

    lax.fori_loop(0, reps - 1, send_rows, 0)

    half = tps // 2
    gather_copy(hidden, sibling, me_t, 0).start()
    for k in range(1, half):
        gather_copy(hidden, tp_at(2 * k), me_t, k).start()

    dispatch = fill(me_r)
    in_rows[me_r] = dot(dispatch[:cap], hidden[...]).astype(BF16)
    in_ids[me_r] = dot(inner, dispatch, NT)

    loads[9].wait()
    diagonal = iota((rows, rows), 0) == iota((rows, rows), 1)
    length_col = jnp.sum(jnp.where(diagonal, lengths[...].astype(F32), 0.0), axis=1, keepdims=True)
    length_v[...] = jnp.broadcast_to(length_col, (rows, HD))

    inverse = 1.0 / HD**0.5
    loads[0].wait()
    loads[1].wait()
    loads[2].wait()
    loads[10].wait()

    def attend(b, c):
        at = pl.ds(pl.multiple_of(b * ROW_BLOCK, ROW_BLOCK), ROW_BLOCK)
        column = iota((ROW_BLOCK, span), 1).astype(F32)
        low = (iota((ROW_BLOCK, span), 0) * positions).astype(F32)
        high = low + length_v[at, 0:1]
        bias = jnp.where((column >= low) & (column < high), 0.0, MASKED)
        lane = iota((ROW_BLOCK, HD), 1)
        own_lanes = jnp.zeros((ROW_BLOCK, HD), F32)
        for g in range(kv_local):
            feats = slice(g * HD, (g + 1) * HD)
            heads = [slice((g * group + j) * HD, (g * group + j + 1) * HD) for j in range(group)]
            query = jnp.concatenate([q_v[at, h] for h in heads], axis=0)
            keys = k_v[at, :, feats].reshape(span, HD)
            values = v_v[at, :, feats].reshape(span, HD)
            scores = dot(query, keys, NT).reshape(group, ROW_BLOCK, span) * inverse + bias[None]
            own = (
                jnp.sum(
                    query.astype(F32).reshape(group, ROW_BLOCK, HD) * fresh[at, feats].astype(F32)[None],
                    axis=-1, keepdims=True,
                )
                * inverse
            )
            top = jnp.maximum(jnp.max(scores, axis=-1, keepdims=True), own)
            expo = jnp.exp(scores - top)
            own_expo = jnp.exp(own - top)
            scale = 1.0 / (jnp.sum(expo, axis=-1, keepdims=True) + own_expo)
            weights = (expo * scale).astype(BF16).reshape(group * ROW_BLOCK, span)
            own_weight = (own_expo * scale).astype(BF16).astype(F32)
            mixed = dot(weights, values)
            for j, h in enumerate(heads):
                mixed_v[at, h] = mixed[j * ROW_BLOCK:(j + 1) * ROW_BLOCK]
                own_lanes = jnp.where(lane == g * group + j, own_weight[j], own_lanes)
        own_v[at, :] = own_lanes
        return c


    def part_copy(k, s):
        return pltpu.make_async_remote_copy(
            src_ref=part.at[s], dst_ref=parts.at[me_t, s], send_sem=part_send.at[k, s],
            recv_sem=part_recv.at[me_t, s], device_id={"tp": tp_at(k)}, device_id_type=pl.DeviceIdType.MESH,
        )

    def part_arrival(k, s):
        q = tp_at(k)
        return pltpu.make_async_remote_copy(
            src_ref=part.at[s], dst_ref=parts.at[q, s], send_sem=part_send.at[k, s],
            recv_sem=part_recv.at[q, s], device_id={"tp": q}, device_id_type=pl.DeviceIdType.MESH,
        )

    def delta_copy(s):
        return pltpu.make_async_remote_copy(
            src_ref=out_delta.at[s], dst_ref=in_delta.at[me_r], send_sem=delta_send.at[s],
            recv_sem=delta_recv.at[me_r], device_id={"rep": s}, device_id_type=pl.DeviceIdType.MESH,
        )

    def delta_arrival(s):
        return pltpu.make_async_remote_copy(
            src_ref=out_delta.at[s], dst_ref=in_delta.at[s], send_sem=delta_send.at[s],
            recv_sem=delta_recv.at[s], device_id={"rep": s}, device_id_type=pl.DeviceIdType.MESH,
        )

    def chosen(s):
        return iota((stored, rank, cap), 0).astype(F32) == in_ids[s][0:1, :cap].reshape(1, 1, cap)

    def shrink(s):
        full = dot(down_v[...], in_rows[s], NT).reshape(stored, rank, cap)
        part[s] = jnp.sum(jnp.where(chosen(s), full, 0.0), axis=0)
        for k in range(1, tps):
            part_copy(k, s).start()

    def expand(s):
        total = part[s]
        for k in range(1, tps):
            part_arrival(k, s).wait_recv()
            total = total + parts[tp_at(k), s]
        total = total.astype(BF16).astype(F32)
        spread = jnp.where(chosen(s), total[None], 0.0).reshape(stored * rank, cap).astype(BF16)
        return (ADAPTER_SCALE * dot(spread, up_v[...], TN)).astype(BF16)

    def forward():
        for k in range(1, half):
            q = tp_at(2 * k)
            gather_copy(hidden, q, q, 0).wait_recv()
            gather_copy(shards.at[q], sibling, q, half + k).start()
        loads[4].wait()
        value_v[...] = dot(hidden[...], w_v[me_t])
        in_delta[me_r] = expand(me_r)

    def finish_base():
        base = value_v[...]
        for k in range(1, half):
            q = tp_at(2 * k)
            base = base + dot(shards[q], w_v[q])
        for k in range(half):
            q = lax.rem(sibling + 2 * k, tps)
            gather_copy(hidden, q, q, 0).wait_recv()
            base = base + dot(shards[q], w_v[q])
        value_v[...] = base + dot(slots[me_r][:cap], in_delta[me_r], TN)

    def step(i, c):
        s = rep_near(i)
        row_arrival(s).wait_recv()
        id_arrival(s).wait_recv()
        shrink(s)
        pl.when(i == 1)(forward)
        pl.when(i == min(2, reps - 1))(finish_base)
        out_delta[s] = expand(s)
        delta_copy(s).start()
        return c

    blocks = rows // ROW_BLOCK
    early = blocks // 2
    lax.fori_loop(0, early, attend, 0)
    loads[3].wait()
    loads[5].wait()
    shrink(me_r)
    lax.fori_loop(early, blocks, attend, 0)

    def send_later(i, c):
        row_copy(rep_near(i)).wait_send()
        row_copy(rep_near(1 + i)).start()
        return c

    lax.fori_loop(direct, reps - 1, send_later, 0)
    lax.fori_loop(1, reps, step, 0)

    def collect(i, c):
        s = rep_near(i)
        delta_arrival(s).wait_recv()
        value_v[...] += dot(slots[s][:cap], in_delta[s], TN)
        return c

    lax.fori_loop(1, reps, collect, 0)

    value_b[...] = value_v[...].astype(BF16)

    gather_copy(hidden, sibling, me_t, 0).wait_send()
    for k in range(1, half):
        gather_copy(hidden, sibling, me_t, k).wait_send()
        gather_copy(hidden, sibling, me_t, half + k).wait_send()

    def drain(i, c):
        d = rep_near(i)
        pl.when((i < direct) | (i == reps - 1))(row_copy(d).wait_send)
        id_copy(d).wait_send()
        delta_copy(d).wait_send()
        return c

    lax.fori_loop(1, reps, drain, 0)

    def drain_parts(s, c):
        for k in range(1, tps):
            part_copy(k, s).wait_send()
        return c

    lax.fori_loop(0, reps, drain_parts, 0)


def combine(value_v, mixed_v, own_v, value_out, attended_out, attended_v, sem):
    kv_local = value_v.shape[1] // HD
    width = mixed_v.shape[1] // kv_local
    stores = [pltpu.make_async_copy(value_v, value_out, sem.at[0])]
    stores[0].start()
    for g in range(kv_local):
        value = value_v[:, g * HD:(g + 1) * HD].astype(F32)
        for j in range(width // HD):
            n = g * (width // HD) + j
            h = slice(n * HD, (n + 1) * HD)
            attended_v[:, h] = (mixed_v[:, h] + own_v[:, n:n + 1] * value).astype(BF16)
        p = slice(g * width, (g + 1) * width)
        stores.append(pltpu.make_async_copy(attended_v.at[:, p], attended_out.at[:, p], sem.at[1 + g]))
        stores[-1].start()
    for store in stores:
        store.wait()


def shards_fn(
    hidden, queries, fresh_token_keys, cached_key_rows, cached_value_rows, lengths, row_adapter_index,
    adapter_table_place, value_projection_matrix, adapter_down_factor, adapter_up_factor,
):
    reps, tps = lax.axis_size("rep"), lax.axis_size("tp")
    rows, width = hidden.shape
    stored, rank, _ = adapter_down_factor.shape
    out_width = adapter_up_factor.shape[2]
    cap = max(2, (2 * rows + reps - 1) // reps)
    dma = pltpu.SemaphoreType.DMA
    vmem = pltpu.VMEM
    w = value_projection_matrix.reshape(tps, width, out_width)
    adapters = adapter_table_place.shape[0]
    scratch = [
        vmem(hidden.shape, BF16), vmem(fresh_token_keys.shape, BF16),
        vmem((1, rows), jnp.int32), vmem((1, rows), jnp.int32), vmem((1, adapters), jnp.int32),
        vmem(queries.shape, BF16), vmem(cached_key_rows.shape, BF16), vmem(cached_value_rows.shape, BF16),
        vmem(w.shape, BF16), vmem((stored * rank, width), BF16), vmem((stored * rank, out_width), BF16), dma((11,)),
        vmem((tps, rows, width), BF16),
        vmem((reps, cap, width), BF16), vmem((reps, cap, width), BF16),
        vmem((reps, 8, rows), F32), vmem((reps, 8, rows), F32),
        vmem((reps, rows, rows), BF16),
        vmem((reps, rank, cap), F32), vmem((tps, reps, rank, cap), F32),
        vmem((reps, cap, out_width), BF16), vmem((reps, cap, out_width), BF16),
        vmem((rows, HD), F32), vmem((rows, out_width), F32),
        dma((tps,)), dma((tps,)), dma((reps,)), dma((reps,)), dma((reps,)), dma((reps,)),
        dma((tps, reps)), dma((tps, reps)), dma((reps,)), dma((reps,)),
    ]
    anywhere, inside = pl.BlockSpec(memory_space=pl.ANY), pl.BlockSpec(memory_space=pltpu.VMEM)
    results = (jax.ShapeDtypeStruct((rows, out_width), BF16), jax.ShapeDtypeStruct(queries.shape, BF16))
    value, mixed, own = pl.pallas_call(
        functools.partial(kernel, reps, tps, cap, stored, rank),
        out_shape=(
            vmem((rows, out_width), BF16), vmem(queries.shape, F32), vmem((rows, HD), F32),
        ),
        in_specs=[anywhere] * 11,
        out_specs=(inside,) * 3,
        scratch_shapes=scratch,
        compiler_params=pltpu.CompilerParams(
            collective_id=0, has_side_effects=True, vmem_limit_bytes=60 * 1024 * 1024
        ),
    )(
        hidden, fresh_token_keys, lengths.reshape(1, rows), row_adapter_index.reshape(1, rows),
        adapter_table_place.reshape(1, -1), queries, cached_key_rows, cached_value_rows, w,
        adapter_down_factor.reshape(stored * rank, width), adapter_up_factor.reshape(stored * rank, out_width),
    )
    return pl.pallas_call(
        combine,
        out_shape=results,
        in_specs=[inside] * 3,
        out_specs=(anywhere, anywhere),
        scratch_shapes=[vmem(queries.shape, BF16), dma((1 + out_width // HD,))],
        compiler_params=pltpu.CompilerParams(vmem_limit_bytes=16 * 1024 * 1024),
    )(value, mixed, own)


def solution(mesh):
    return jax.shard_map(
        shards_fn,
        mesh=mesh,
        in_specs=(
            P(("groups", "rep"), "tp"),
            P(("groups", "rep"), "tp"),
            P(("groups", "rep"), "tp"),
            P(("groups", "rep"), None, "tp"),
            P(("groups", "rep"), None, "tp"),
            P(("groups", "rep")),
            P(("groups", "rep")),
            P("groups"),
            P(None, "tp"),
            P(("groups", "rep"), None, "tp"),
            P(("groups", "rep"), None, "tp"),
        ),
        out_specs=(P(("groups", "rep"), "tp"), P(("groups", "rep"), "tp")),
        check_vma=False,
    )
```

```python
import functools

import jax
import jax.numpy as jnp
from jax import lax
from jax.experimental import pallas as pl
from jax.experimental.pallas import tpu as pltpu
from jax.sharding import PartitionSpec as P

HD = 128
ROW_BLOCK = 16
ADAPTER_SCALE = 2.0
MASKED = -1e30
F32, BF16 = jnp.float32, jnp.bfloat16
NT = (((1,), (1,)), ((), ()))
TN = (((0,), (0,)), ((), ()))
NN = (((1,), (0,)), ((), ()))


def dot(a, b, dims=NN):
    return lax.dot_general(a, b, dims, preferred_element_type=F32)


def iota(shape, dim):
    return lax.broadcasted_iota(jnp.int32, shape, dim)


def kernel(
    reps, tps, cap, stored, rank,
    hidden_hbm, fresh_hbm, lengths_hbm, index_hbm, places_hbm, q_hbm, k_hbm, v_hbm, w_hbm, down_hbm, up_hbm,
    value_b, mixed_v, own_v,
    hidden, fresh, lengths, index, places,
    q_v, k_v, v_v, w_v, down_v, up_v, local_sem,
    shards, out_rows, in_rows, out_ids, in_ids, slots, part, parts, out_delta, in_delta,
    length_v, value_v,
    gather_send, gather_recv, row_send, row_recv, id_send, id_recv,
    part_send, part_recv, delta_send, delta_recv,
):
    me_r, me_t = lax.axis_index("rep"), lax.axis_index("tp")
    rows, kv_local = hidden.shape[0], fresh.shape[1] // HD
    group = q_v.shape[1] // fresh.shape[1]
    positions = k_v.shape[1]
    span = ROW_BLOCK * positions

    def rep_at(k):
        return lax.rem(me_r + k, reps)

    rep_sibling = me_r + 1 - 2 * lax.rem(me_r, 2)

    def rep_near(i):
        odd = lax.rem(i, 2)
        return lax.rem(odd * rep_sibling + (1 - odd) * me_r + 2 * (i // 2), reps)

    def tp_at(k):
        return lax.rem(me_t + k, tps)

    sibling = me_t + 1 - 2 * lax.rem(me_t, 2)

    loads = [
        pltpu.make_async_copy(src, dst, local_sem.at[n])
        for n, (src, dst) in enumerate(
            (
                (q_hbm, q_v), (k_hbm, k_v), (v_hbm, v_v), (down_hbm, down_v), (w_hbm, w_v), (up_hbm, up_v),
                (index_hbm, index), (places_hbm, places), (hidden_hbm, hidden), (lengths_hbm, lengths), (fresh_hbm, fresh),
            )
        )
    ]
    for n in (6, 7, 8):
        loads[n].start()

    barrier = pltpu.get_barrier_semaphore()

    def greet_rep(k, c):
        pl.semaphore_signal(barrier, inc=1, device_id={"rep": rep_at(k)}, device_id_type=pl.DeviceIdType.MESH)
        return c

    def greet_tp(k, c):
        pl.semaphore_signal(barrier, inc=1, device_id={"tp": tp_at(k)}, device_id_type=pl.DeviceIdType.MESH)
        return c

    lax.fori_loop(1, reps, greet_rep, 0)
    lax.fori_loop(1, tps, greet_tp, 0)

    loads[6].wait()
    loads[7].wait()
    adapters = places.shape[1]
    place = places[...].astype(F32)
    owner_tab = jnp.floor((place + 0.5) / stored)
    inner_tab = place - owner_tab * stored
    hot = (iota((adapters, rows), 0) == index[...]).astype(F32).astype(BF16)
    owner = dot(jnp.broadcast_to(owner_tab, (8, adapters)).astype(BF16), hot)
    inner = dot(jnp.broadcast_to(inner_tab, (8, adapters)).astype(BF16), hot).astype(BF16)
    rep_pad = max(8, reps)
    owner_row = owner[0:1, :]
    owner_hot = (iota((rep_pad, rows), 0).astype(F32) == owner_row).astype(F32)
    earlier = (iota((rows, rows), 0) < iota((rows, rows), 1)).astype(F32).astype(BF16)
    before = dot(owner_hot.astype(BF16), earlier)
    position = jnp.sum(before * owner_hot, axis=0, keepdims=True)
    slot_iota = iota((rows, rows), 0).astype(F32)

    def gather_copy(src, to, q, n):
        return pltpu.make_async_remote_copy(
            src_ref=src, dst_ref=shards.at[q], send_sem=gather_send.at[n], recv_sem=gather_recv.at[q],
            device_id={"tp": to}, device_id_type=pl.DeviceIdType.MESH,
        )

    def row_copy(d):
        return pltpu.make_async_remote_copy(
            src_ref=out_rows.at[d], dst_ref=in_rows.at[me_r], send_sem=row_send.at[d], recv_sem=row_recv.at[me_r],
            device_id={"rep": d}, device_id_type=pl.DeviceIdType.MESH,
        )

    def id_copy(d):
        return pltpu.make_async_remote_copy(
            src_ref=out_ids.at[d], dst_ref=in_ids.at[me_r], send_sem=id_send.at[d], recv_sem=id_recv.at[me_r],
            device_id={"rep": d}, device_id_type=pl.DeviceIdType.MESH,
        )

    def row_arrival(s):
        return pltpu.make_async_remote_copy(
            src_ref=out_rows.at[s], dst_ref=in_rows.at[s], send_sem=row_send.at[s], recv_sem=row_recv.at[s],
            device_id={"rep": s}, device_id_type=pl.DeviceIdType.MESH,
        )

    def id_arrival(s):
        return pltpu.make_async_remote_copy(
            src_ref=out_ids.at[s], dst_ref=in_ids.at[s], send_sem=id_send.at[s], recv_sem=id_recv.at[s],
            device_id={"rep": s}, device_id_type=pl.DeviceIdType.MESH,
        )

    def fill(d):
        member = jnp.where(owner_row == d.astype(F32), position, -1.0)
        dispatch = (slot_iota == member).astype(F32).astype(BF16)
        slots[d] = dispatch
        return dispatch

    loads[8].wait()
    for n in (9, 10, 0, 1, 2, 3, 5, 4):
        loads[n].start()
    pl.semaphore_wait(barrier, reps - 1 + tps - 1)

    direct = reps // 2

    def send_rows(i, c):
        d = rep_near(jnp.where(i < direct, direct - i, 1 + i))
        dispatch = fill(d)
        out_rows[d] = dot(dispatch[:cap], hidden[...]).astype(BF16)
        pl.when(i < direct)(row_copy(d).start)
        out_ids[d] = dot(inner, dispatch, NT)
        id_copy(d).start()
        return c

    lax.fori_loop(0, reps - 1, send_rows, 0)

    half = tps // 2
    gather_copy(hidden, sibling, me_t, 0).start()
    for k in range(1, half):
        gather_copy(hidden, tp_at(2 * k), me_t, k).start()

    dispatch = fill(me_r)
    in_rows[me_r] = dot(dispatch[:cap], hidden[...]).astype(BF16)
    in_ids[me_r] = dot(inner, dispatch, NT)

    loads[9].wait()
    diagonal = iota((rows, rows), 0) == iota((rows, rows), 1)
    length_col = jnp.sum(jnp.where(diagonal, lengths[...].astype(F32), 0.0), axis=1, keepdims=True)
    length_v[...] = jnp.broadcast_to(length_col, (rows, HD))

    inverse = 1.0 / HD**0.5
    loads[0].wait()
    loads[1].wait()
    loads[2].wait()
    loads[10].wait()

    def attend(b, c):
        at = pl.ds(pl.multiple_of(b * ROW_BLOCK, ROW_BLOCK), ROW_BLOCK)
        column = iota((ROW_BLOCK, span), 1).astype(F32)
        low = (iota((ROW_BLOCK, span), 0) * positions).astype(F32)
        high = low + length_v[at, 0:1]
        bias = jnp.where((column >= low) & (column < high), 0.0, MASKED)
        lane = iota((ROW_BLOCK, HD), 1)
        own_lanes = jnp.zeros((ROW_BLOCK, HD), F32)
        for g in range(kv_local):
            feats = slice(g * HD, (g + 1) * HD)
            heads = [slice((g * group + j) * HD, (g * group + j + 1) * HD) for j in range(group)]
            query = jnp.concatenate([q_v[at, h] for h in heads], axis=0)
            keys = k_v[at, :, feats].reshape(span, HD)
            values = v_v[at, :, feats].reshape(span, HD)
            scores = dot(query, keys, NT).reshape(group, ROW_BLOCK, span) * inverse + bias[None]
            own = (
                jnp.sum(
                    query.astype(F32).reshape(group, ROW_BLOCK, HD) * fresh[at, feats].astype(F32)[None],
                    axis=-1, keepdims=True,
                )
                * inverse
            )
            top = jnp.maximum(jnp.max(scores, axis=-1, keepdims=True), own)
            expo = jnp.exp(scores - top)
            own_expo = jnp.exp(own - top)
            scale = 1.0 / (jnp.sum(expo, axis=-1, keepdims=True) + own_expo)
            weights = (expo * scale).astype(BF16).reshape(group * ROW_BLOCK, span)
            own_weight = (own_expo * scale).astype(BF16).astype(F32)
            mixed = dot(weights, values)
            for j, h in enumerate(heads):
                mixed_v[at, h] = mixed[j * ROW_BLOCK:(j + 1) * ROW_BLOCK]
                own_lanes = jnp.where(lane == g * group + j, own_weight[j], own_lanes)
        own_v[at, :] = own_lanes
        return c


    def part_copy(k, s):
        return pltpu.make_async_remote_copy(
            src_ref=part.at[s], dst_ref=parts.at[me_t, s], send_sem=part_send.at[k, s],
            recv_sem=part_recv.at[me_t, s], device_id={"tp": tp_at(k)}, device_id_type=pl.DeviceIdType.MESH,
        )

    def part_arrival(k, s):
        q = tp_at(k)
        return pltpu.make_async_remote_copy(
            src_ref=part.at[s], dst_ref=parts.at[q, s], send_sem=part_send.at[k, s],
            recv_sem=part_recv.at[q, s], device_id={"tp": q}, device_id_type=pl.DeviceIdType.MESH,
        )

    def delta_copy(s):
        return pltpu.make_async_remote_copy(
            src_ref=out_delta.at[s], dst_ref=in_delta.at[me_r], send_sem=delta_send.at[s],
            recv_sem=delta_recv.at[me_r], device_id={"rep": s}, device_id_type=pl.DeviceIdType.MESH,
        )

    def delta_arrival(s):
        return pltpu.make_async_remote_copy(
            src_ref=out_delta.at[s], dst_ref=in_delta.at[s], send_sem=delta_send.at[s],
            recv_sem=delta_recv.at[s], device_id={"rep": s}, device_id_type=pl.DeviceIdType.MESH,
        )

    def chosen(s):
        return iota((stored, rank, cap), 0).astype(F32) == in_ids[s][0:1, :cap].reshape(1, 1, cap)

    def shrink(s):
        full = dot(down_v[...], in_rows[s], NT).reshape(stored, rank, cap)
        part[s] = jnp.sum(jnp.where(chosen(s), full, 0.0), axis=0)
        for k in range(tps - 1, 0, -1):
            part_copy(k, s).start()

    def expand(s):
        total = part[s]
        for k in range(1, tps):
            part_arrival(k, s).wait_recv()
            total = total + parts[tp_at(k), s]
        total = total.astype(BF16).astype(F32)
        spread = jnp.where(chosen(s), total[None], 0.0).reshape(stored * rank, cap).astype(BF16)
        return (ADAPTER_SCALE * dot(spread, up_v[...], TN)).astype(BF16)

    def forward():
        for k in range(1, half):
            q = tp_at(2 * k)
            gather_copy(hidden, q, q, 0).wait_recv()
            gather_copy(shards.at[q], sibling, q, half + k).start()
        loads[4].wait()
        value_v[...] = dot(hidden[...], w_v[me_t])
        in_delta[me_r] = expand(me_r)

    def finish_base():
        base = value_v[...]
        for k in range(1, half):
            q = tp_at(2 * k)
            base = base + dot(shards[q], w_v[q])
        for k in range(half):
            q = lax.rem(sibling + 2 * k, tps)
            gather_copy(hidden, q, q, 0).wait_recv()
            base = base + dot(shards[q], w_v[q])
        value_v[...] = base + dot(slots[me_r][:cap], in_delta[me_r], TN)

    def turn(i, c):
        s = rep_near(i)
        slots[s] = jnp.transpose(slots[s].astype(F32)).astype(BF16)
        return c

    def step(i, c):
        s = rep_near(i)
        row_arrival(s).wait_recv()
        id_arrival(s).wait_recv()
        shrink(s)
        pl.when(i == 1)(forward)
        pl.when(i == min(2, reps - 1))(finish_base)
        turn(i, c)
        out_delta[s] = expand(s)
        delta_copy(s).start()
        return c

    blocks = rows // ROW_BLOCK
    early = blocks // 2
    lax.fori_loop(0, early, attend, 0)
    loads[3].wait()
    loads[5].wait()
    shrink(me_r)
    lax.fori_loop(early, blocks, attend, 0)

    def send_later(i, c):
        row_copy(rep_near(i)).wait_send()
        row_copy(rep_near(1 + i)).start()
        return c

    lax.fori_loop(direct, reps - 1, send_later, 0)
    lax.fori_loop(1, reps, step, 0)

    def collect(i, c):
        s = rep_near(i)
        delta_arrival(s).wait_recv()
        value_v[...] += dot(slots[s][:, :cap], in_delta[s])
        return c

    lax.fori_loop(1, reps, collect, 0)

    value_b[...] = value_v[...].astype(BF16)

    gather_copy(hidden, sibling, me_t, 0).wait_send()
    for k in range(1, half):
        gather_copy(hidden, sibling, me_t, k).wait_send()
        gather_copy(hidden, sibling, me_t, half + k).wait_send()

    def drain(i, c):
        d = rep_near(i)
        pl.when((i < direct) | (i == reps - 1))(row_copy(d).wait_send)
        id_copy(d).wait_send()
        delta_copy(d).wait_send()
        return c

    lax.fori_loop(1, reps, drain, 0)

    def drain_parts(s, c):
        for k in range(1, tps):
            part_copy(k, s).wait_send()
        return c

    lax.fori_loop(0, reps, drain_parts, 0)


def combine(value_v, mixed_v, own_v, value_out, attended_out, attended_v, sem):
    kv_local = value_v.shape[1] // HD
    width = mixed_v.shape[1] // kv_local
    stores = [pltpu.make_async_copy(value_v, value_out, sem.at[0])]
    stores[0].start()
    for g in range(kv_local):
        value = value_v[:, g * HD:(g + 1) * HD].astype(F32)
        for j in range(width // HD):
            n = g * (width // HD) + j
            h = slice(n * HD, (n + 1) * HD)
            attended_v[:, h] = (mixed_v[:, h] + own_v[:, n:n + 1] * value).astype(BF16)
        p = slice(g * width, (g + 1) * width)
        stores.append(pltpu.make_async_copy(attended_v.at[:, p], attended_out.at[:, p], sem.at[1 + g]))
        stores[-1].start()
    for store in stores:
        store.wait()


def shards_fn(
    hidden, queries, fresh_token_keys, cached_key_rows, cached_value_rows, lengths, row_adapter_index,
    adapter_table_place, value_projection_matrix, adapter_down_factor, adapter_up_factor,
):
    reps, tps = lax.axis_size("rep"), lax.axis_size("tp")
    rows, width = hidden.shape
    stored, rank, _ = adapter_down_factor.shape
    out_width = adapter_up_factor.shape[2]
    cap = max(2, (2 * rows + reps - 1) // reps)
    dma = pltpu.SemaphoreType.DMA
    vmem = pltpu.VMEM
    w = value_projection_matrix.reshape(tps, width, out_width)
    adapters = adapter_table_place.shape[0]
    scratch = [
        vmem(hidden.shape, BF16), vmem(fresh_token_keys.shape, BF16),
        vmem((1, rows), jnp.int32), vmem((1, rows), jnp.int32), vmem((1, adapters), jnp.int32),
        vmem(queries.shape, BF16), vmem(cached_key_rows.shape, BF16), vmem(cached_value_rows.shape, BF16),
        vmem(w.shape, BF16), vmem((stored * rank, width), BF16), vmem((stored * rank, out_width), BF16), dma((11,)),
        vmem((tps, rows, width), BF16),
        vmem((reps, cap, width), BF16), vmem((reps, cap, width), BF16),
        vmem((reps, 8, rows), F32), vmem((reps, 8, rows), F32),
        vmem((reps, rows, rows), BF16),
        vmem((reps, rank, cap), F32), vmem((tps, reps, rank, cap), F32),
        vmem((reps, cap, out_width), BF16), vmem((reps, cap, out_width), BF16),
        vmem((rows, HD), F32), vmem((rows, out_width), F32),
        dma((tps,)), dma((tps,)), dma((reps,)), dma((reps,)), dma((reps,)), dma((reps,)),
        dma((tps, reps)), dma((tps, reps)), dma((reps,)), dma((reps,)),
    ]
    anywhere, inside = pl.BlockSpec(memory_space=pl.ANY), pl.BlockSpec(memory_space=pltpu.VMEM)
    results = (jax.ShapeDtypeStruct((rows, out_width), BF16), jax.ShapeDtypeStruct(queries.shape, BF16))
    value, mixed, own = pl.pallas_call(
        functools.partial(kernel, reps, tps, cap, stored, rank),
        out_shape=(
            vmem((rows, out_width), BF16), vmem(queries.shape, F32), vmem((rows, HD), F32),
        ),
        in_specs=[anywhere] * 11,
        out_specs=(inside,) * 3,
        scratch_shapes=scratch,
        compiler_params=pltpu.CompilerParams(
            collective_id=0, has_side_effects=True, vmem_limit_bytes=60 * 1024 * 1024
        ),
    )(
        hidden, fresh_token_keys, lengths.reshape(1, rows), row_adapter_index.reshape(1, rows),
        adapter_table_place.reshape(1, -1), queries, cached_key_rows, cached_value_rows, w,
        adapter_down_factor.reshape(stored * rank, width), adapter_up_factor.reshape(stored * rank, out_width),
    )
    return pl.pallas_call(
        combine,
        out_shape=results,
        in_specs=[inside] * 3,
        out_specs=(anywhere, anywhere),
        scratch_shapes=[vmem(queries.shape, BF16), dma((1 + out_width // HD,))],
        compiler_params=pltpu.CompilerParams(vmem_limit_bytes=16 * 1024 * 1024),
    )(value, mixed, own)


def solution(mesh):
    return jax.shard_map(
        shards_fn,
        mesh=mesh,
        in_specs=(
            P(("groups", "rep"), "tp"),
            P(("groups", "rep"), "tp"),
            P(("groups", "rep"), "tp"),
            P(("groups", "rep"), None, "tp"),
            P(("groups", "rep"), None, "tp"),
            P(("groups", "rep")),
            P(("groups", "rep")),
            P("groups"),
            P(None, "tp"),
            P(("groups", "rep"), None, "tp"),
            P(("groups", "rep"), None, "tp"),
        ),
        out_specs=(P(("groups", "rep"), "tp"), P(("groups", "rep"), "tp")),
        check_vma=False,
    )
```
